128 devices in a mesh: dp: 8 (over z, y_lo), ctx: 16 (over y_hi, x, core).
Axes of the slice: x: 4, y: 4 (y_hi: 2, y_lo: 2; y = y_hi * 2 + y_lo), z: 4, core: 2. Of those that a mesh axis runs over, the one named last changes fastest.
Arguments:
- queries: bfloat16 [8, 2048, 8192], P('dp', 'ctx'), may hold values from -6 to 6
- keys: bfloat16 [8, 2048, 8192], P('dp', 'ctx'), may hold values from -6 to 6
- values: bfloat16 [8, 2048, 8192], P('dp', 'ctx'), may hold values from -6 to 6
- out_grad: bfloat16 [8, 2048, 8192], P('dp', 'ctx'), may hold values from -6 to 6
- residue: float32 [16, 8192], P(None, 'ctx'), may hold values from -0.12 to 0.12
- rate: float32 [16, 8192], P(None, 'ctx'), may hold values from 0.00024414062 to 0.05
Outputs:
- query_grad: bfloat16 [8, 2048, 8192], P('dp', 'ctx')
- key_grad: bfloat16 [8, 2048, 8192], P('dp', 'ctx')
- value_grad: bfloat16 [8, 2048, 8192], P('dp', 'ctx')
- residue_grad: float32 [16, 8192], P(None, 'ctx')
- rate_grad: float32 [16, 8192], P(None, 'ctx')
The draws below stay inside these ranges and needn't reach their ends.
All inputs are finite; a program needn't handle non-finite values.
Results may differ from the reference program's by a relative error of at most 0.017.
Values may be sent and summed in bfloat16 or wider, within the bound.
No kernel may reach another device: no remote copies, remote signals or barrier semaphores. Data moves between devices by JAX's collectives and lax.ppermute only.
A program may use at most 128 MiB of HBM per device.

```python
import math
import jax
import jax.numpy as jnp
from jax import lax

D = 8192
MODES = 16
SEQLEN = 2048
BATCH = 8


def level_of(rng, dims, pieces, smallest, largest):
    def one(dim, blocks):
        draws = jax.random.uniform(jax.random.fold_in(jax.random.fold_in(rng, 6), dim), (blocks,), jnp.float32, smallest / len(pieces), largest / len(pieces))
        return jnp.repeat(jnp.exp(draws), dims[dim] // blocks).reshape((-1,) + (1,) * (len(dims) - dim - 1))

    factor_of = one(*pieces[0])
    for cut in pieces[1:]:
        factor_of = factor_of * one(*cut)
    return factor_of


def scatter_about(rng, extent, deviation, limit, split=(), held_as=jnp.bfloat16):
    array = deviation * jax.random.normal(rng, extent, jnp.float32)
    if split:
        array = array * level_of(rng, extent, split, -0.22, 0.18)
    return jnp.clip(array, -limit, limit).astype(held_as)


def setup_inputs(seed: int = 0) -> dict:
    streams_of = jax.random.split(jax.random.key(seed), 7)
    queries = scatter_about(streams_of[0], (BATCH, SEQLEN, D), 1.0, 6.0, ((0, 8), (1, 16)))
    keys = scatter_about(streams_of[1], (BATCH, SEQLEN, D), 1.0, 6.0, ((0, 8), (1, 16)))
    values = scatter_about(streams_of[2], (BATCH, SEQLEN, D), 1.0, 6.0, ((0, 8), (1, 16)))
    out_grad = scatter_about(streams_of[3], (BATCH, SEQLEN, D), 1.0, 6.0, ((0, 8), (1, 16)))
    residue = scatter_about(streams_of[4], (MODES, D), 0.02, 0.12, ((1, 16),), jnp.float32)
    rate = jnp.clip(jnp.exp(math.log(0.05) - 5.322034 * jax.random.uniform(streams_of[5], (MODES, D), jnp.float32) ** level_of(streams_of[5], (MODES, D), ((1, 16),), -0.2, 0.2)), 0.00024414062, 0.05)
    return {"queries": queries, "keys": keys, "values": values, "out_grad": out_grad, "residue": residue, "rate": rate}


exact_mode = lax.Precision.HIGHEST


def angle_table(row_count, col_count, period):
    product = (jnp.arange(row_count, dtype=jnp.int32)[:, None] * jnp.arange(col_count, dtype=jnp.int32)[None, :]) % period
    phase_angle = product.astype(jnp.float32) * (2.0 * math.pi / period)
    return (jnp.cos(phase_angle), -jnp.sin(phase_angle))


def make_tables(full_len):
    outer = full_len // 64
    first_cos, first_sin = angle_table(outer, outer // 2, outer)
    twist_cos, twist_sin = angle_table(outer, 64, full_len)
    inner_cos, inner_sin = angle_table(64, 64, 64)
    return (first_cos.astype(jnp.bfloat16), first_sin.astype(jnp.bfloat16), twist_cos, twist_sin,
            inner_cos.astype(jnp.bfloat16), inner_sin.astype(jnp.bfloat16))


def wide_einsum(form, left, right):
    return jnp.einsum(form, left.astype(jnp.float32), right.astype(jnp.float32), precision=exact_mode)


def forward_dft(signal, tables):
    first_cos, first_sin, twist_cos, twist_sin, inner_cos, inner_sin = tables
    part_real = wide_einsum('ka,batc->bktc', first_cos, signal)
    part_imag = wide_einsum('ka,batc->bktc', first_sin, signal)
    turn_cos = twist_cos[None, :, :, None]
    turn_sin = twist_sin[None, :, :, None]
    turned_real = (part_real * turn_cos - part_imag * turn_sin).astype(jnp.bfloat16)
    turned_imag = (part_real * turn_sin + part_imag * turn_cos).astype(jnp.bfloat16)
    out_real = wide_einsum('bktc,tj->bkjc', turned_real, inner_cos) - wide_einsum('bktc,tj->bkjc', turned_imag, inner_sin)
    out_imag = wide_einsum('bktc,tj->bkjc', turned_real, inner_sin) + wide_einsum('bktc,tj->bkjc', turned_imag, inner_cos)
    return out_real, out_imag


def inverse_dft(spec_real, spec_imag, tables, full_len):
    first_cos, first_sin, twist_cos, twist_sin, inner_cos, inner_sin = tables
    spec_real = spec_real.astype(jnp.bfloat16)
    spec_imag = spec_imag.astype(jnp.bfloat16)
    back_real = wide_einsum('bkjc,tj->bktc', spec_real, inner_cos) + wide_einsum('bkjc,tj->bktc', spec_imag, inner_sin)
    back_imag = wide_einsum('bkjc,tj->bktc', spec_imag, inner_cos) - wide_einsum('bkjc,tj->bktc', spec_real, inner_sin)
    turn_cos = twist_cos[None, :, :, None]
    turn_sin = twist_sin[None, :, :, None]
    turned_real = (back_real * turn_cos + back_imag * turn_sin).astype(jnp.bfloat16)
    turned_imag = (back_imag * turn_cos - back_real * turn_sin).astype(jnp.bfloat16)
    signal = wide_einsum('ka,bktc->batc', first_cos, turned_real) + wide_einsum('ka,bktc->batc', first_sin, turned_imag)
    return signal / full_len


def reference(queries, keys, values, out_grad, residue, rate):
    batch_count = queries.shape[0]
    seq_len = queries.shape[1]
    full_len = 2 * seq_len
    half_rows = seq_len // 64
    tables = make_tables(full_len)
    gated = (out_grad.astype(jnp.float32) * queries.astype(jnp.float32)).astype(jnp.bfloat16)
    mixed = (keys.astype(jnp.float32) * values.astype(jnp.float32)).astype(jnp.bfloat16)
    lags = jnp.arange(seq_len).astype(jnp.float32).reshape(half_rows, 64)
    chan_block = min(256, D)
    block_count = D // chan_block

    def channel_slab(number):
        start = (number * chan_block).astype(jnp.int32)
        gate_part = lax.dynamic_slice_in_dim(gated, start, chan_block, 2).reshape(batch_count, half_rows, 64, chan_block)
        mix_part = lax.dynamic_slice_in_dim(mixed, start, chan_block, 2).reshape(batch_count, half_rows, 64, chan_block)
        res_part = lax.dynamic_slice_in_dim(residue, start, chan_block, 1)
        rate_part = lax.dynamic_slice_in_dim(rate, start, chan_block, 1)
        decays = jnp.exp(-rate_part[:, None, None, :] * lags[None, :, :, None])
        filt = jnp.sum(res_part[:, None, None, :] * decays, 0).astype(jnp.bfloat16)
        filt_real, filt_imag = forward_dft(filt[None], tables)
        mix_real, mix_imag = forward_dft(mix_part, tables)
        gate_real, gate_imag = forward_dft(gate_part, tables)
        conv = inverse_dft(filt_real * mix_real - filt_imag * mix_imag,
                           filt_real * mix_imag + filt_imag * mix_real, tables, full_len)
        back = inverse_dft(filt_real * gate_real + filt_imag * gate_imag,
                           filt_real * gate_imag - filt_imag * gate_real, tables, full_len)
        lagged = inverse_dft(mix_real * gate_real + mix_imag * gate_imag,
                             mix_real * gate_imag - mix_imag * gate_real, tables, full_len)
        lagged = jnp.sum(lagged, 0)
        res_grad = jnp.sum(lagged[None] * decays, (1, 2))
        rate_grad = -res_part * jnp.sum(lags[None, :, :, None] * lagged[None] * decays, (1, 2))
        conv = conv.astype(jnp.bfloat16).reshape(batch_count, seq_len, chan_block)
        back = back.astype(jnp.bfloat16).reshape(batch_count, seq_len, chan_block)
        return conv, back, res_grad, rate_grad

    conv, back, res_grad, rate_grad = lax.map(channel_slab, jnp.arange(block_count, dtype=jnp.int32))
    conv = jnp.transpose(conv, (1, 2, 0, 3)).reshape(queries.shape)
    back = jnp.transpose(back, (1, 2, 0, 3)).reshape(queries.shape)
    res_grad = jnp.transpose(res_grad, (1, 0, 2)).reshape(residue.shape)
    rate_grad = jnp.transpose(rate_grad, (1, 0, 2)).reshape(rate.shape)
    query_grad = (out_grad.astype(jnp.float32) * conv.astype(jnp.float32)).astype(jnp.bfloat16)
    key_grad = (back.astype(jnp.float32) * values.astype(jnp.float32)).astype(jnp.bfloat16)
    value_grad = (back.astype(jnp.float32) * keys.astype(jnp.float32)).astype(jnp.bfloat16)
    return (query_grad, key_grad, value_grad, res_grad, rate_grad)
```

```python
import jax
import jax.numpy as jnp
from jax import lax
from jax.experimental import pallas as pl
from jax.experimental.pallas import tpu as pltpu
from jax.sharding import PartitionSpec as P

LEN = 128
MODES = 16
GROUP = 1024
F32 = jnp.float32
BF16 = jnp.bfloat16


def params(vmem=32):
    return pltpu.CompilerParams(vmem_limit_bytes=vmem * 1024 * 1024)


def cost(ops, moved):
    return pl.CostEstimate(flops=ops, bytes_accessed=moved, transcendentals=0)


def product(left, right):
    return (left.astype(F32) * right.astype(F32)).astype(BF16)


def gate_kernel(keys, values, out_grad, queries, x_out, g_out):
    for j in range(8):
        lanes = pl.ds(128 * j, 128)
        rows = pl.ds(j, LEN, stride=8)
        x_out[rows, :] = product(keys[:, lanes], values[:, lanes]).astype(F32)
        g_out[rows, :] = product(out_grad[:, lanes], queries[:, lanes]).astype(F32)


def spread(block, scratch, base=0):
    for m in range(MODES):
        for h in range(2):
            scratch[pl.ds(8 * m + 4 * h, 4), :] = block[h, pl.ds(base + 4 * m, 4), :]


def decays(rate, scratch):
    spread(rate, scratch)
    scratch[...] = jnp.exp(-scratch[...])


def modes_of(scratch, first=0, count=MODES):
    return tuple(scratch[pl.ds(8 * m, 8), :] for m in range(first, first + count))


def gather_rows(out, base, mode, state):
    for h in range(2):
        out[h, pl.ds(base + 4 * mode, 4), :] = state[4 * h : 4 * h + 4]


def row(t):
    return pl.ds(pl.multiple_of(8 * t, 8), 8)


def state_kernel(rate, x, g, out, lam_s):
    decays(rate, lam_s)
    lam = modes_of(lam_s)
    zero = jnp.zeros((8, 128), F32)

    def step(t, carry):
        fwd, bwd = carry
        xt = x[row(t), :]
        gt = g[row(LEN - 1 - t), :]
        fwd = tuple(l * s + xt for l, s in zip(lam, fwd))
        bwd = tuple(l * s + gt for l, s in zip(lam, bwd))
        return fwd, bwd

    fwd, bwd = lax.fori_loop(0, LEN, step, ((zero,) * MODES, (zero,) * MODES), unroll=2)
    for m in range(MODES):
        gather_rows(out, 0, m, fwd[m])
        gather_rows(out, 64, m, bwd[m])


def grad_kernel(rate, x, g, out, lam_s, wide):
    decays(rate, lam_s)
    zero = jnp.zeros((8, 128), F32)
    part = 8
    for first in range(0, MODES, part):
        lam = modes_of(lam_s, first, part)

        def step(t, carry):
            h, p, hg, pg = carry
            xt = x[row(t), :]
            gt = g[row(t), :]
            q = tuple(l * s for l, s in zip(lam, h))
            h = tuple(s + xt for s in q)
            p = tuple(l * s + u for l, s, u in zip(lam, p, q))
            hg = tuple(s + gt * u for s, u in zip(hg, h))
            pg = tuple(s + gt * u for s, u in zip(pg, p))
            return h, p, hg, pg

        h, p, hg, pg = lax.fori_loop(0, LEN, step, ((zero,) * part,) * 4, unroll=2)
        for m in range(part):
            gather_rows(wide, 0, first + m, p[m])
            gather_rows(wide, 128, first + m, hg[m])
            gather_rows(wide, 192, first + m, pg[m])
    lam = modes_of(lam_s)

    def back_step(t, carry):
        a, b = carry
        gt = g[row(LEN - 1 - t), :]
        q = tuple(l * s for l, s in zip(lam, a))
        a = tuple(s + gt for s in q)
        b = tuple(l * s + u for l, s, u in zip(lam, b, q))
        return a, b

    a, b = lax.fori_loop(0, LEN, back_step, ((zero,) * MODES,) * 2, unroll=2)
    for m in range(MODES):
        gather_rows(wide, 64, m, b[m])
    out[...] = wide[...].astype(BF16)


def total(terms):
    terms = list(terms)
    while len(terms) > 1:
        terms = [u + v for u, v in zip(terms[::2], terms[1::2])]
    return terms[0]


def local_kernel(rate, residue, x, g, conv, back, lam_s, res_s):
    decays(rate, lam_s)
    spread(residue, res_s)
    lam = modes_of(lam_s)
    res = modes_of(res_s)
    zero = jnp.zeros((8, 128), F32)

    def run(source, target, place):
        def step(t, h):
            at = row(place(t))
            xt = source[at, :]
            h = tuple(l * s + xt for l, s in zip(lam, h))
            target[at, :] = total(r * s for r, s in zip(res, h))
            return h

        lax.fori_loop(0, LEN, step, (zero,) * MODES, unroll=2)

    run(x, conv, lambda t: t)
    run(g, back, lambda t: LEN - 1 - t)


def scan_kernel(sums, rate, residue, out):
    lam = jnp.exp(-rate[...])
    far = jnp.exp(-float(LEN) * rate[...])
    scale = residue[...] * lam
    count = sums.shape[0]
    state = jnp.zeros((64, 128), F32)
    for d in range(count):
        out[d, 0:64, :] = scale * state
        state = far * state + sums[d, 0:64, :]
    state = jnp.zeros((64, 128), F32)
    for d in range(count - 1, -1, -1):
        out[d, 64:128, :] = scale * state
        state = far * state + sums[d, 64:128, :]


def owner_grad_kernel(sums, parts, rate, residue, out):
    lam = jnp.exp(-rate[...])
    far = jnp.exp(-float(LEN) * rate[...])
    zero = jnp.zeros((64, 128), F32)
    h, q, hg, pg, hb, qb = zero, zero, zero, zero, zero, zero
    for d in range(sums.shape[0]):
        b = sums[d, 64:128, :]
        hg = hg + parts[d, 128:192, :].astype(F32)
        pg = pg + parts[d, 192:256, :].astype(F32)
        hb = hb + h * b
        qb = qb + h * (parts[d, 64:128, :].astype(F32) + b) + q * b
        q = far * (q + float(LEN) * h) + parts[d, 0:64, :].astype(F32)
        h = far * h + sums[d, 0:64, :]
    out[0:64, :] = hg + lam * hb
    out[64:128, :] = -residue[...] * (pg + lam * qb)


def finish_kernel(rate, ends, conv, back, out_grad, keys, values, query_out, key_out, value_out, lam_s, head_s, tail_s, conv_s, back_s):
    decays(rate, lam_s)
    spread(ends, head_s)
    spread(ends, tail_s, 64)
    lam = modes_of(lam_s)

    def step(t, carry):
        head, tail = carry
        up, down = row(t), row(LEN - 1 - t)
        conv_s[up, :] = conv[up, :] + total(head)
        back_s[down, :] = back[down, :] + total(tail)
        return tuple(l * s for l, s in zip(lam, head)), tuple(l * s for l, s in zip(lam, tail))

    lax.fori_loop(0, LEN, step, (modes_of(head_s), modes_of(tail_s)), unroll=2)
    for j in range(8):
        lanes = pl.ds(128 * j, 128)
        rows = pl.ds(j, LEN, stride=8)
        c = conv_s[rows, :].astype(BF16)
        b = back_s[rows, :].astype(BF16)
        query_out[:, lanes] = product(out_grad[:, lanes], c)
        key_out[:, lanes] = product(b, values[:, lanes])
        value_out[:, lanes] = product(b, keys[:, lanes])


def wide_spec():
    return pl.BlockSpec((LEN, GROUP), lambda p: (0, p))


def tall_spec():
    return pl.BlockSpec((GROUP, 128), lambda p: (p, 0))


def owner_spec(rows):
    return pl.BlockSpec((2, rows, 128), lambda p: (p, 0, 0))


def registers(count):
    return pltpu.VMEM((8 * count, 128), F32)


def exchange(array):
    return lax.all_to_all(array, "ctx", split_axis=0, concat_axis=0, tiled=True)


def body(queries, keys, values, out_grad, residue, rate):
    owners = 16
    chans = queries.shape[2]
    groups = chans // GROUP
    flat = [a.reshape(LEN, chans) for a in (keys, values, out_grad, queries)]
    tall = jax.ShapeDtypeStruct((groups * GROUP, 128), F32)
    work = LEN * chans * MODES
    rate_own = rate.reshape(64, 128)
    residue_own = residue.reshape(64, 128)
    rate_all = exchange(jnp.broadcast_to(rate_own[None], (owners, 64, 128)))
    x, g = pl.pallas_call(
        gate_kernel,
        grid=(groups,),
        in_specs=[wide_spec()] * 4,
        out_specs=[tall_spec()] * 2,
        out_shape=[tall, tall],
        compiler_params=params(),
        cost_estimate=cost(LEN * chans * 4, LEN * chans * 16),
        name="gate",
    )(*flat)
    sums = pl.pallas_call(
        state_kernel,
        grid=(groups,),
        in_specs=[owner_spec(64), tall_spec(), tall_spec()],
        out_specs=owner_spec(128),
        out_shape=jax.ShapeDtypeStruct((owners, 128, 128), F32),
        scratch_shapes=[registers(MODES)],
        compiler_params=params(),
        cost_estimate=cost(4 * work, LEN * chans * 8),
        name="states",
    )(rate_all, x, g)
    sums_own = exchange(sums)
    residue_all = exchange(jnp.broadcast_to(residue_own[None], (owners, 64, 128)))
    parts = pl.pallas_call(
        grad_kernel,
        grid=(groups,),
        in_specs=[owner_spec(64), tall_spec(), tall_spec()],
        out_specs=owner_spec(256),
        out_shape=jax.ShapeDtypeStruct((owners, 256, 128), BF16),
        scratch_shapes=[registers(MODES), pltpu.VMEM((2, 256, 128), F32)],
        compiler_params=params(),
        cost_estimate=cost(12 * work, LEN * chans * 8),
        name="local_grads",
    )(rate_all, x, g)
    ends_own = pl.pallas_call(
        scan_kernel,
        out_shape=jax.ShapeDtypeStruct((owners, 128, 128), F32),
        compiler_params=params(),
        name="scan",
    )(sums_own, rate_own, residue_own)
    ends = exchange(ends_own)
    parts_own = exchange(parts)
    conv, back = pl.pallas_call(
        local_kernel,
        grid=(groups,),
        in_specs=[owner_spec(64), owner_spec(64), tall_spec(), tall_spec()],
        out_specs=[tall_spec()] * 2,
        out_shape=[tall, tall],
        scratch_shapes=[registers(MODES)] * 2,
        compiler_params=params(),
        cost_estimate=cost(8 * work, LEN * chans * 16),
        name="local_conv",
    )(rate_all, residue_all, x, g)
    grads = pl.pallas_call(
        owner_grad_kernel,
        out_shape=jax.ShapeDtypeStruct((128, 128), F32),
        compiler_params=params(),
        name="owner_grads",
    )(sums_own, parts_own, rate_own, residue_own)
    for bit in (1, 2, 4):
        grads = grads + lax.ppermute(grads, "dp", [(i, i ^ bit) for i in range(8)])
    flat_out = jax.ShapeDtypeStruct((LEN, chans), BF16)
    query_grad, key_grad, value_grad = pl.pallas_call(
        finish_kernel,
        grid=(groups,),
        in_specs=[owner_spec(64), owner_spec(128), tall_spec(), tall_spec()] + [wide_spec()] * 3,
        out_specs=[wide_spec()] * 3,
        out_shape=[flat_out] * 3,
        scratch_shapes=[registers(MODES)] * 3 + [pltpu.VMEM((GROUP, 128), F32)] * 2,
        compiler_params=params(),
        cost_estimate=cost(4 * work, LEN * chans * 20),
        name="finish",
    )(rate_all, ends, conv, back, flat[2], flat[0], flat[1])
    shape = queries.shape
    return (
        query_grad.reshape(shape),
        key_grad.reshape(shape),
        value_grad.reshape(shape),
        grads[:64].reshape(residue.shape),
        grads[64:].reshape(rate.shape),
    )


def solution(mesh):
    wide = P("dp", "ctx", None)
    narrow = P(None, "ctx")
    return jax.shard_map(
        body,
        mesh=mesh,
        in_specs=(wide,) * 4 + (narrow,) * 2,
        out_specs=(wide,) * 3 + (narrow,) * 2,
        check_vma=False,
    )
```

```python
import math

import jax
import jax.numpy as jnp
import ml_dtypes
import numpy as np
from jax import lax
from jax.experimental import pallas as pl
from jax.experimental.pallas import tpu as pltpu
from jax.sharding import PartitionSpec as P

HALF = 128
LEN = 256
STEPS = LEN // 8
MODES = 16
WIDTH = 512
BLOCKS = 8
TOGETHER = 4
PART = 256
F32 = jnp.float32
BF16 = jnp.bfloat16


def tables():
    angle = math.pi * np.outer(2 * np.arange(LEN) + 1, np.arange(LEN)) / (2 * LEN)
    forward = np.concatenate([np.cos(angle), -np.sin(angle)], 0)
    inverse = forward.T / LEN
    return forward.astype(ml_dtypes.bfloat16), inverse.astype(ml_dtypes.bfloat16)


def params(vmem=63):
    return pltpu.CompilerParams(vmem_limit_bytes=vmem * 1024 * 1024)


def cost(ops, moved):
    return pl.CostEstimate(flops=ops, bytes_accessed=moved, transcendentals=0)


def product(left, right):
    return (left.astype(F32) * right.astype(F32)).astype(BF16)


def total(terms):
    terms = list(terms)
    while len(terms) > 1:
        terms = [u + v for u, v in zip(terms[::2], terms[1::2])]
    return terms[0]


def copies_kernel(array, out):
    for d in range(out.shape[0]):
        out[d] = array[...]


def gate_kernel(core, keys, values, out_grad, queries, x_keep, g_keep, x_give, g_give):
    even = core[0] == 0
    for left, right, keep, give in ((keys, values, x_keep, x_give), (out_grad, queries, g_keep, g_give)):
        for q in range(keep.shape[1] // WIDTH):
            first = pl.ds(2 * q * WIDTH, WIDTH)
            second = pl.ds((2 * q + 1) * WIDTH, WIDTH)
            u = product(left[:, first], right[:, first])
            v = product(left[:, second], right[:, second])
            keep[:, pl.ds(q * WIDTH, WIDTH)] = jnp.where(even, u, v)
            give[:, pl.ds(q * WIDTH, WIDTH)] = jnp.where(even, v, u)


def ladder(width, flip=False):
    s = lax.broadcasted_iota(jnp.int32, (8, width), 0).astype(F32)
    return 7.0 - s if flip else s


def column(values):
    return jnp.sum(values, axis=0, keepdims=True)


def power_sums(rates, signals, lanes):
    y = [jnp.broadcast_to(jnp.exp(-8.0 * rate), (8, 128)) for rate in rates]
    power = list(y)

    def load(ref, back, k):
        return ref[pl.ds(LEN - 8 - 8 * k if back else 8 * k, 8), lanes]

    v = [[load(ref, back, 0)] * len(rates) for ref, back in signals]
    d = [list(u) for u in v]
    for k in range(1, STEPS):
        for i, (ref, back) in enumerate(signals):
            sk = load(ref, back, k)
            for j in range(len(rates)):
                v[i][j] = v[i][j] + power[j] * sk
                if k < STEPS - 1:
                    d[i][j] = d[i][j] + v[i][j]
        if k < STEPS - 1:
            power = [p * u for p, u in zip(power, y)]
    last = float(STEPS - 1)
    return [[(vj, last * vj - dj) for vj, dj in zip(vi, di)] for vi, di in zip(v, d)]


def state_kernel(core, prm, residue, x_keep, g_keep, x_got, g_got, x_out, g_out, sums, parts, x_s, g_s, sums_s):
    low = pl.multiple_of(core[0] * HALF, HALF)
    high = pl.multiple_of(HALF - core[0] * HALF, HALF)
    for keep, got, out, wide in ((x_keep, x_got, x_out, x_s), (g_keep, g_got, g_out, g_s)):
        for part, at in ((keep, low), (got, high)):
            block = part[...]
            out[pl.ds(at, HALF), :] = block
            wide[pl.ds(at, HALF), :] = block.astype(F32)
    for tile in range(WIDTH // 128):
        lanes = pl.ds(128 * tile, 128)
        s, r = ladder(128), ladder(128, True)

        def some(group, carry):
            modes = [TOGETHER * group + i for i in range(TOGETHER)]
            rates = [prm[0, pl.ds(m, 1), lanes] for m in modes]
            xs = power_sums(rates, ((x_s, True), (g_s, False)), lanes)
            for m, rate, (v, d) in zip(modes, rates, xs[0]):
                weight = jnp.exp(-rate * r)
                sums[0, pl.ds(m, 1), lanes] = column(weight * v)
                sums_s[pl.ds(m, 1), lanes] = column(weight * (8.0 * d + r * v))
            for m, rate, (v, d) in zip(modes, rates, xs[1]):
                weight = jnp.exp(-rate * s)
                sums[0, pl.ds(MODES + m, 1), lanes] = column(weight * v)
                sums_s[pl.ds(MODES + m, 1), lanes] = column(weight * (8.0 * d + s * v))
            return carry

        lax.fori_loop(0, MODES // TOGETHER, some, 0, unroll=True)
    parts[0] = sums_s[...].astype(BF16)
    sums[0, 2 * MODES : 3 * MODES, :] = residue[...]


def dft(table, signal):
    return jnp.dot(table, signal, preferred_element_type=F32)


def correlate(forward, inverse, left, right):
    lr, li, rr, ri = left[:LEN], left[LEN:], right[:LEN], right[LEN:]
    both = jnp.concatenate([(lr * rr + li * ri).astype(BF16), (lr * ri - li * rr).astype(BF16)], 0)
    return dft(inverse, both)


def convolve(forward, inverse, left, right):
    lr, li, rr, ri = left[:LEN], left[LEN:], right[:LEN], right[LEN:]
    both = jnp.concatenate([(lr * rr - li * ri).astype(BF16), (lr * ri + li * rr).astype(BF16)], 0)
    return dft(inverse, both)


def grad_kernel(prm, forward, inverse, x, g, parts, lag_s, sums_s):
    fwd, inv = forward[...], inverse[...]
    for part in range(WIDTH // PART):
        lanes = pl.ds(PART * part, PART)
        lag_s[:, lanes] = correlate(fwd, inv, dft(fwd, x[:, lanes]), dft(fwd, g[:, lanes]))
    for tile in range(WIDTH // 128):
        lanes = pl.ds(128 * tile, 128)
        s = ladder(128)

        def some(group, carry):
            modes = [TOGETHER * group + i for i in range(TOGETHER)]
            rates = [prm[0, pl.ds(m, 1), lanes] for m in modes]
            (lags,) = power_sums(rates, ((lag_s, False),), lanes)
            for m, rate, (v, d) in zip(modes, rates, lags):
                weight = jnp.exp(-rate * s)
                sums_s[pl.ds(m, 1), lanes] = column(weight * v)
                sums_s[pl.ds(MODES + m, 1), lanes] = column(weight * (8.0 * d + s * v))
            return carry

        lax.fori_loop(0, MODES // TOGETHER, some, 0, unroll=True)
    parts[0] = sums_s[...].astype(BF16)


def expand(rates, heads, flip, put):
    for tile in range(WIDTH // 128):
        lanes = slice(128 * tile, 128 * tile + 128)
        s = ladder(128, flip)
        y = tuple(jnp.broadcast_to(jnp.exp(-8.0 * rates[m : m + 1, lanes]), (8, 128)) for m in range(MODES))
        z = tuple(heads[m : m + 1, lanes] * jnp.exp(-rates[m : m + 1, lanes] * s) for m in range(MODES))
        for k in range(STEPS):
            put(k, lanes, total(z))
            if k < STEPS - 1:
                z = tuple(u * v for u, v in zip(z, y))


def local_kernel(prm, residue, forward, inverse, x, g, conv, back, filt_s):
    fwd, inv = forward[...], inverse[...]

    def put(k, lanes, rows):
        filt_s[pl.ds(8 * k, 8), lanes] = rows

    expand(prm[0], residue[0], False, put)
    for part in range(WIDTH // PART):
        lanes = pl.ds(PART * part, PART)
        filt = dft(fwd, filt_s[:, lanes].astype(BF16))
        conv[:, lanes] = convolve(fwd, inv, filt, dft(fwd, x[:, lanes]))
        back[:, lanes] = correlate(fwd, inv, filt, dft(fwd, g[:, lanes]))


def scan_kernel(sums, grad_a, grad_b, own_rate, residue, out):
    rate = own_rate[...]
    scale = residue[...] * jnp.exp(-rate)
    far = jnp.exp(-float(LEN) * rate)

    def write(d, base, state):
        ends = scale * state
        near = ends.astype(BF16)
        out[d, base : base + MODES, :] = near
        out[d, base + MODES : base + 2 * MODES, :] = (ends - near.astype(F32)).astype(BF16)

    state = jnp.zeros((MODES, WIDTH), F32)
    for d in range(BLOCKS):
        write(d, 0, state)
        state = far * state + sums[d, 0:MODES, :]
    state = jnp.zeros((MODES, WIDTH), F32)
    for d in range(BLOCKS - 1, -1, -1):
        write(d, 2 * MODES, state)
        state = far * state + sums[d, MODES : 2 * MODES, :]
    for d in range(BLOCKS):
        out[d, 64:96, :] = grad_a[d]
        out[d, 96:128, :] = grad_b[d]


def owner_grad_kernel(sums, got, own_rate, residue, out):
    rate = own_rate[...]
    lam = jnp.exp(-rate)
    far = jnp.exp(-float(LEN) * rate)
    zero = jnp.zeros((MODES, WIDTH), F32)
    h, q, hg, pg, hb, qb = zero, zero, zero, zero, zero, zero
    for d in range(BLOCKS):
        b = sums[d, MODES : 2 * MODES, :]
        p, w, hd, pd = (got[d, 64 + 16 * i : 80 + 16 * i, :].astype(F32) for i in range(4))
        hg = hg + hd
        pg = pg + pd
        hb = hb + h * b
        qb = qb + h * (w + b) + q * b
        q = far * (q + float(LEN) * h) + p
        h = far * h + sums[d, 0:MODES, :]
    first = hg + lam * hb
    second = -residue[...] * (pg + lam * qb)
    for b in range(out.shape[0]):
        out[b, 0:MODES, :] = first
        out[b, MODES : 2 * MODES, :] = second


def finish_kernel(core, prm, ends, conv, back, conv_keep, back_keep, conv_give, back_give, conv_s, back_s):
    rates = prm[0]
    head = ends[0, 0:16, :].astype(F32) + ends[0, 16:32, :].astype(F32)
    tail = ends[0, 32:48, :].astype(F32) + ends[0, 48:64, :].astype(F32)

    def put_conv(k, lanes, rows):
        at = pl.ds(8 * k, 8)
        conv_s[at, lanes] = conv[at, lanes] + rows

    def put_back(k, lanes, rows):
        at = pl.ds(LEN - 8 - 8 * k, 8)
        back_s[at, lanes] = back[at, lanes] + rows

    expand(rates, head, False, put_conv)
    expand(rates, tail, True, put_back)
    mine = pl.multiple_of(core[0] * HALF, HALF)
    other = pl.multiple_of(HALF - core[0] * HALF, HALF)
    for scratch, keep, give in ((conv_s, conv_keep, conv_give), (back_s, back_keep, back_give)):
        keep[...] = scratch[pl.ds(mine, HALF), :].astype(BF16)
        give[...] = scratch[pl.ds(other, HALF), :].astype(BF16)


def out_kernel(core, out_grad, keys, values, conv_keep, back_keep, conv_got, back_got, query_out, key_out, value_out):
    even = core[0] == 0
    for q in range(conv_keep.shape[1] // WIDTH):
        at = pl.ds(q * WIDTH, WIDTH)
        for h in range(2):
            lanes = pl.ds((2 * q + h) * WIDTH, WIDTH)
            c, b = (
                jnp.where(even, u[:, at], v[:, at]) if h == 0 else jnp.where(even, v[:, at], u[:, at])
                for u, v in ((conv_keep, conv_got), (back_keep, back_got))
            )
            query_out[:, lanes] = product(out_grad[:, lanes], c)
            key_out[:, lanes] = product(b, values[:, lanes])
            value_out[:, lanes] = product(b, keys[:, lanes])


def call(kernel, name, work, grid, in_specs, out_specs, shapes, scratch, operands, prefetch=True):
    spec = pltpu.PrefetchScalarGridSpec(
        num_scalar_prefetch=1 if prefetch else 0, grid=grid, in_specs=in_specs, out_specs=out_specs, scratch_shapes=scratch
    )
    return pl.pallas_call(
        kernel, grid_spec=spec, out_shape=shapes, compiler_params=params(), cost_estimate=work, name=name
    )(*operands)


def swap(array):
    return lax.ppermute(array, "ctx", [(i, i ^ 1) for i in range(2 * BLOCKS)])


def exchange(array):
    groups = [[2 * q + c for q in range(BLOCKS)] for c in range(2)]
    return lax.all_to_all(array, "ctx", split_axis=0, concat_axis=0, axis_index_groups=groups, tiled=True)


def body(queries, keys, values, out_grad, residue, rate):
    chans = queries.shape[2]
    half = chans // 2
    queries2, keys2, values2, out_grad2 = (a.reshape(HALF, chans) for a in (queries, keys, values, out_grad))
    core = (lax.axis_index("ctx") % 2).astype(jnp.int32).reshape(1)
    prm = exchange(
        pl.pallas_call(
            copies_kernel,
            out_shape=jax.ShapeDtypeStruct((BLOCKS, MODES, WIDTH), F32),
            compiler_params=params(),
            name="rate_copies",
        )(rate)
    )
    forward, inverse = tables()
    work = LEN * half * MODES
    moved = LEN * half

    part = pl.BlockSpec((HALF, WIDTH), lambda q, *_: (0, q))
    whole = pl.BlockSpec((LEN, WIDTH), lambda q, *_: (0, q))
    own = pl.BlockSpec((MODES, WIDTH), lambda q, *_: (0, 0))
    rows16 = pl.BlockSpec((1, MODES, WIDTH), lambda q, *_: (q, 0, 0))
    rows48 = pl.BlockSpec((1, 48, WIDTH), lambda q, *_: (q, 0, 0))
    residues = pl.BlockSpec((1, MODES, WIDTH), lambda q, *_: (q, 2, 0))
    rows32 = pl.BlockSpec((1, 32, WIDTH), lambda q, *_: (q, 0, 0))
    rows64 = pl.BlockSpec((1, 64, WIDTH), lambda q, *_: (q, 0, 0))
    table_f = pl.BlockSpec((2 * LEN, LEN), lambda q, *_: (0, 0))
    table_i = pl.BlockSpec((LEN, 2 * LEN), lambda q, *_: (0, 0))
    shape_part = jax.ShapeDtypeStruct((HALF, half), BF16)
    shape_whole = jax.ShapeDtypeStruct((LEN, half), BF16)
    shape_wide = jax.ShapeDtypeStruct((LEN, half), F32)
    shape_rows = jax.ShapeDtypeStruct((BLOCKS, 32, WIDTH), BF16)
    wide = pltpu.VMEM((LEN, WIDTH), F32)
    narrow = pltpu.VMEM((32, WIDTH), F32)

    pair = pl.BlockSpec((HALF, 4 * WIDTH), lambda q, *_: (0, q))
    pair_half = pl.BlockSpec((HALF, 2 * WIDTH), lambda q, *_: (0, q))
    x_keep, g_keep, x_give, g_give = call(
        gate_kernel, "gate", cost(2 * moved, 12 * moved), (BLOCKS // 2,), [pair] * 4, [pair_half] * 4, [shape_part] * 4, [],
        (core, keys2, values2, out_grad2, queries2),
    )
    x_give, g_give, prm = lax.optimization_barrier((x_give, g_give, prm))
    x_got, g_got = swap(x_give), swap(g_give)
    x, g, sums, grad_a = call(
        state_kernel, "states", cost(7 * work, 8 * moved), (BLOCKS,), [rows16, own] + [part] * 4,
        [whole, whole, rows48, rows32],
        [shape_whole, shape_whole, jax.ShapeDtypeStruct((BLOCKS, 48, WIDTH), F32), shape_rows],
        [wide, wide, narrow], (core, prm, residue, x_keep, g_keep, x_got, g_got),
    )
    sums_own = exchange(sums)
    grad_b = call(
        grad_kernel, "local_grads", cost(6 * work, 4 * moved), (BLOCKS,), [rows16, table_f, table_i, whole, whole],
        rows32, shape_rows, [wide, narrow], (prm, forward, inverse, x, g), False,
    )
    ends_own = pl.pallas_call(
        scan_kernel,
        out_shape=jax.ShapeDtypeStruct((BLOCKS, 128, WIDTH), BF16),
        compiler_params=params(),
        name="scan",
    )(sums_own, grad_a, grad_b, rate, residue)
    ends = exchange(ends_own)
    conv, back = call(
        local_kernel, "local_conv", cost(5 * work, 12 * moved), (BLOCKS,), [rows16, residues, table_f, table_i, whole, whole],
        [whole, whole], [shape_wide, shape_wide], [wide], (prm, sums_own, forward, inverse, x, g), False,
    )
    grads = pl.pallas_call(
        owner_grad_kernel,
        out_shape=jax.ShapeDtypeStruct((8, 32, WIDTH), F32),
        compiler_params=params(),
        name="owner_grads",
    )(sums_own, ends, rate, residue)
    grads, ends = lax.optimization_barrier((grads, ends))
    grads = lax.all_to_all(grads, "dp", split_axis=0, concat_axis=0, tiled=True)
    grads = jnp.sum(grads, 0)
    conv_keep, back_keep, conv_give, back_give = call(
        finish_kernel, "finish", cost(4 * work, 12 * moved), (BLOCKS,), [rows16, rows64, whole, whole], [part] * 4,
        [shape_part] * 4, [wide, wide], (core, prm, ends, conv, back),
    )
    conv_give, back_give, grads = lax.optimization_barrier((conv_give, back_give, grads))
    conv_got, back_got = swap(conv_give), swap(back_give)
    shape_out = jax.ShapeDtypeStruct((HALF, chans), BF16)
    outs = call(
        out_kernel, "outputs", cost(3 * moved, 16 * moved), (BLOCKS // 2,), [pair] * 3 + [pair_half] * 4, [pair] * 3,
        [shape_out] * 3, [], (core, out_grad2, keys2, values2, conv_keep, back_keep, conv_got, back_got),
    )
    query_grad, key_grad, value_grad = (a.reshape(queries.shape) for a in outs)
    return query_grad, key_grad, value_grad, grads[:MODES], grads[MODES:]


def solution(mesh):
    wide = P("dp", "ctx", None)
    narrow = P(None, "ctx")
    return jax.shard_map(
        body,
        mesh=mesh,
        in_specs=(wide,) * 4 + (narrow,) * 2,
        out_specs=(wide,) * 3 + (narrow,) * 2,
        check_vma=False,
    )
```

```python
import math

import jax
import jax.numpy as jnp
import ml_dtypes
import numpy as np
from jax import lax
from jax.experimental import pallas as pl
from jax.experimental.pallas import tpu as pltpu
from jax.sharding import PartitionSpec as P

HALF = 128
LEN = 256
STEPS = LEN // 8
MODES = 16
WIDTH = 512
BLOCKS = 8
TOGETHER = 4
PART = 256
F32 = jnp.float32
BF16 = jnp.bfloat16


def tables():
    angle = math.pi * np.outer(2 * np.arange(LEN) + 1, np.arange(LEN)) / (2 * LEN)
    forward = np.concatenate([np.cos(angle), -np.sin(angle)], 0)
    inverse = forward.T / LEN
    return forward.astype(ml_dtypes.bfloat16), inverse.astype(ml_dtypes.bfloat16)


def params(vmem=63):
    return pltpu.CompilerParams(vmem_limit_bytes=vmem * 1024 * 1024)


def cost(ops, moved):
    return pl.CostEstimate(flops=ops, bytes_accessed=moved, transcendentals=0)


def product(left, right):
    return (left.astype(F32) * right.astype(F32)).astype(BF16)


def total(terms):
    terms = list(terms)
    while len(terms) > 1:
        terms = [u + v for u, v in zip(terms[::2], terms[1::2])]
    return terms[0]


def copies_kernel(array, out):
    for d in range(out.shape[0]):
        out[d] = array[...]


def gate_kernel(core, keys, values, out_grad, queries, x_keep, g_keep, x_give, g_give):
    even = core[0] == 0
    for left, right, keep, give in ((keys, values, x_keep, x_give), (out_grad, queries, g_keep, g_give)):
        for q in range(keep.shape[1] // WIDTH):
            first = pl.ds(2 * q * WIDTH, WIDTH)
            second = pl.ds((2 * q + 1) * WIDTH, WIDTH)
            u = product(left[:, first], right[:, first])
            v = product(left[:, second], right[:, second])
            keep[:, pl.ds(q * WIDTH, WIDTH)] = jnp.where(even, u, v)
            give[:, pl.ds(q * WIDTH, WIDTH)] = jnp.where(even, v, u)


def ladder(width, flip=False):
    s = lax.broadcasted_iota(jnp.int32, (8, width), 0).astype(F32)
    return 7.0 - s if flip else s


def column(values):
    return jnp.sum(values, axis=0, keepdims=True)


def power_sums(rates, signals, lanes):
    y = [jnp.broadcast_to(jnp.exp(-8.0 * rate), (8, 128)) for rate in rates]
    power = list(y)

    def load(ref, back, k):
        return ref[pl.ds(LEN - 8 - 8 * k if back else 8 * k, 8), lanes]

    v = [[load(ref, back, 0)] * len(rates) for ref, back in signals]
    d = [list(u) for u in v]
    for k in range(1, STEPS):
        for i, (ref, back) in enumerate(signals):
            sk = load(ref, back, k)
            for j in range(len(rates)):
                v[i][j] = v[i][j] + power[j] * sk
                if k < STEPS - 1:
                    d[i][j] = d[i][j] + v[i][j]
        if k < STEPS - 1:
            power = [p * u for p, u in zip(power, y)]
    last = float(STEPS - 1)
    return [[(vj, last * vj - dj) for vj, dj in zip(vi, di)] for vi, di in zip(v, d)]


def state_kernel(core, prm, residue, x_keep, g_keep, x_got, g_got, x_out, g_out, sums, parts, x_s, g_s, sums_s):
    low = pl.multiple_of(core[0] * HALF, HALF)
    high = pl.multiple_of(HALF - core[0] * HALF, HALF)
    for keep, got, out, wide in ((x_keep, x_got, x_out, x_s), (g_keep, g_got, g_out, g_s)):
        for part, at in ((keep, low), (got, high)):
            block = part[...]
            out[pl.ds(at, HALF), :] = block
            wide[pl.ds(at, HALF), :] = block.astype(F32)
    for tile in range(WIDTH // 128):
        lanes = pl.ds(128 * tile, 128)
        s, r = ladder(128), ladder(128, True)

        def some(group, carry):
            modes = [TOGETHER * group + i for i in range(TOGETHER)]
            rates = [prm[0, pl.ds(m, 1), lanes] for m in modes]
            xs = power_sums(rates, ((x_s, True), (g_s, False)), lanes)
            for m, rate, (v, d) in zip(modes, rates, xs[0]):
                weight = jnp.exp(-rate * r)
                sums[0, pl.ds(m, 1), lanes] = column(weight * v)
                sums_s[pl.ds(m, 1), lanes] = column(weight * (8.0 * d + r * v))
            for m, rate, (v, d) in zip(modes, rates, xs[1]):
                weight = jnp.exp(-rate * s)
                sums[0, pl.ds(MODES + m, 1), lanes] = column(weight * v)
                sums_s[pl.ds(MODES + m, 1), lanes] = column(weight * (8.0 * d + s * v))
            return carry

        lax.fori_loop(0, MODES // TOGETHER, some, 0, unroll=True)
    parts[0] = sums_s[...].astype(BF16)
    sums[0, 2 * MODES : 3 * MODES, :] = residue[...]


def dft(table, signal):
    return jnp.dot(table, signal, preferred_element_type=F32)


def correlate(forward, inverse, left, right):
    lr, li, rr, ri = left[:LEN], left[LEN:], right[:LEN], right[LEN:]
    both = jnp.concatenate([(lr * rr + li * ri).astype(BF16), (lr * ri - li * rr).astype(BF16)], 0)
    return dft(inverse, both)


def convolve(forward, inverse, left, right):
    lr, li, rr, ri = left[:LEN], left[LEN:], right[:LEN], right[LEN:]
    both = jnp.concatenate([(lr * rr - li * ri).astype(BF16), (lr * ri + li * rr).astype(BF16)], 0)
    return dft(inverse, both)


def grad_kernel(prm, forward, inverse, x, g, parts, lag_s, sums_s):
    fwd, inv = forward[...], inverse[...]
    for part in range(WIDTH // PART):
        lanes = pl.ds(PART * part, PART)
        lag_s[:, lanes] = correlate(fwd, inv, dft(fwd, x[:, lanes]), dft(fwd, g[:, lanes]))
    for tile in range(WIDTH // 128):
        lanes = pl.ds(128 * tile, 128)
        s = ladder(128)

        def some(group, carry):
            modes = [TOGETHER * group + i for i in range(TOGETHER)]
            rates = [prm[0, pl.ds(m, 1), lanes] for m in modes]
            (lags,) = power_sums(rates, ((lag_s, False),), lanes)
            for m, rate, (v, d) in zip(modes, rates, lags):
                weight = jnp.exp(-rate * s)
                sums_s[pl.ds(m, 1), lanes] = column(weight * v)
                sums_s[pl.ds(MODES + m, 1), lanes] = column(weight * (8.0 * d + s * v))
            return carry

        lax.fori_loop(0, MODES // TOGETHER, some, 0, unroll=True)
    parts[0] = sums_s[...].astype(BF16)


def expand(minus, steps, heads, flip, put, count):
    for tile in range(WIDTH // 128):
        lanes = pl.ds(128 * tile, 128)
        s = ladder(128, flip)
        y = tuple(jnp.broadcast_to(steps[pl.ds(m, 1), lanes], (8, 128)) for m in range(MODES))
        z = tuple(heads[pl.ds(m, 1), lanes] * jnp.exp(minus[pl.ds(m, 1), lanes] * s) for m in range(MODES))
        for k in range(count):
            put(k, lanes, total(z))
            if k < count - 1:
                z = tuple(u * v for u, v in zip(z, y))


def local_kernel(core, prm, residue, forward, inverse, x, g, conv_keep, back_keep, conv_give, back_give, filt_s, minus_s, step_s, res_s):
    fwd, inv = forward[...], inverse[...]
    even = core[0] == 0
    minus_s[...] = -prm[0]
    step_s[...] = jnp.exp(-8.0 * prm[0])
    res_s[...] = residue[0]

    def put(k, lanes, rows):
        filt_s[pl.ds(8 * k, 8), lanes] = rows

    expand(minus_s, step_s, res_s, False, put, STEPS)
    for part in range(WIDTH // PART):
        lanes = pl.ds(PART * part, PART)
        filt = dft(fwd, filt_s[:, lanes].astype(BF16))
        conv = convolve(fwd, inv, filt, dft(fwd, x[:, lanes])).astype(BF16)
        back = correlate(fwd, inv, filt, dft(fwd, g[:, lanes])).astype(BF16)
        for both, keep, give in ((conv, conv_keep, conv_give), (back, back_keep, back_give)):
            keep[:, lanes] = jnp.where(even, both[:HALF], both[HALF:])
            give[:, lanes] = jnp.where(even, both[HALF:], both[:HALF])


def scan_kernel(sums, grad_a, grad_b, own_rate, residue, out):
    rate = own_rate[...]
    scale = residue[...] * jnp.exp(-rate)
    far = jnp.exp(-float(LEN) * rate)

    def write(d, base, state):
        ends = scale * state
        near = ends.astype(BF16)
        out[d, base : base + MODES, :] = near
        out[d, base + MODES : base + 2 * MODES, :] = (ends - near.astype(F32)).astype(BF16)

    state = jnp.zeros((MODES, WIDTH), F32)
    for d in range(BLOCKS):
        write(d, 0, state)
        state = far * state + sums[d, 0:MODES, :]
    state = jnp.zeros((MODES, WIDTH), F32)
    for d in range(BLOCKS - 1, -1, -1):
        write(d, 2 * MODES, state)
        state = far * state + sums[d, MODES : 2 * MODES, :]
    for d in range(BLOCKS):
        out[d, 64:96, :] = grad_a[d]
        out[d, 96:128, :] = grad_b[d]


def owner_grad_kernel(sums, got, own_rate, residue, out):
    rate = own_rate[...]
    lam = jnp.exp(-rate)
    far = jnp.exp(-float(LEN) * rate)
    zero = jnp.zeros((MODES, WIDTH), F32)
    h, q, hg, pg, hb, qb = zero, zero, zero, zero, zero, zero
    for d in range(BLOCKS):
        b = sums[d, MODES : 2 * MODES, :]
        p, w, hd, pd = (got[d, 16 * i : 16 * i + 16, :].astype(F32) for i in range(4))
        hg = hg + hd
        pg = pg + pd
        hb = hb + h * b
        qb = qb + h * (w + b) + q * b
        q = far * (q + float(LEN) * h) + p
        h = far * h + sums[d, 0:MODES, :]
    first = hg + lam * hb
    second = -residue[...] * (pg + lam * qb)
    for b in range(out.shape[0]):
        out[b, 0:MODES, :] = first
        out[b, MODES : 2 * MODES, :] = second


def finish_kernel(
    core, prm, prm_got, ends, ends_got, conv_keep, back_keep, conv_got, back_got, out_grad, keys, values,
    query_out, key_out, value_out, minus_s, step_s, head_s, tail_s, conv_s, back_s,
):
    upper = core[0].astype(F32) * float(HALF)
    for h in range(2):
        mine = core[0] == h
        minus = -jnp.where(mine, prm[0], prm_got[0])
        edge = jnp.where(mine, ends[0], ends_got[0]).astype(F32)
        minus_s[h] = minus
        step_s[h] = jnp.exp(8.0 * minus)
        head_s[h] = (edge[0:16] + edge[16:32]) * jnp.exp(minus * upper)
        tail_s[h] = (edge[32:48] + edge[48:64]) * jnp.exp(minus * (float(HALF) - upper))

        def put_conv(k, lanes, rows):
            conv_s[h, pl.ds(8 * k, 8), lanes] = rows

        def put_back(k, lanes, rows):
            back_s[h, pl.ds(HALF - 8 - 8 * k, 8), lanes] = rows

        expand(minus_s.at[h], step_s.at[h], head_s.at[h], False, put_conv, HALF // 8)
        expand(minus_s.at[h], step_s.at[h], tail_s.at[h], True, put_back, HALF // 8)
        c = (jnp.where(mine, conv_keep[...], conv_got[...]).astype(F32) + conv_s[h]).astype(BF16)
        b = (jnp.where(mine, back_keep[...], back_got[...]).astype(F32) + back_s[h]).astype(BF16)
        lanes = pl.ds(h * WIDTH, WIDTH)
        query_out[:, lanes] = product(out_grad[:, lanes], c)
        key_out[:, lanes] = product(b, values[:, lanes])
        value_out[:, lanes] = product(b, keys[:, lanes])


def call(kernel, name, work, grid, in_specs, out_specs, shapes, scratch, operands, prefetch=True):
    spec = pltpu.PrefetchScalarGridSpec(
        num_scalar_prefetch=1 if prefetch else 0, grid=grid, in_specs=in_specs, out_specs=out_specs, scratch_shapes=scratch
    )
    return pl.pallas_call(
        kernel, grid_spec=spec, out_shape=shapes, compiler_params=params(), cost_estimate=work, name=name
    )(*operands)


def swap(array):
    return lax.ppermute(array, "ctx", [(i, i ^ 1) for i in range(2 * BLOCKS)])


def exchange(array):
    groups = [[2 * q + c for q in range(BLOCKS)] for c in range(2)]
    return lax.all_to_all(array, "ctx", split_axis=0, concat_axis=0, axis_index_groups=groups, tiled=True)


def body(queries, keys, values, out_grad, residue, rate):
    chans = queries.shape[2]
    half = chans // 2
    queries2, keys2, values2, out_grad2 = (a.reshape(HALF, chans) for a in (queries, keys, values, out_grad))
    core = (lax.axis_index("ctx") % 2).astype(jnp.int32).reshape(1)
    prm = exchange(
        pl.pallas_call(
            copies_kernel,
            out_shape=jax.ShapeDtypeStruct((BLOCKS, MODES, WIDTH), F32),
            compiler_params=params(),
            name="rate_copies",
        )(rate)
    )
    forward, inverse = tables()
    work = LEN * half * MODES
    moved = LEN * half

    part = pl.BlockSpec((HALF, WIDTH), lambda q, *_: (0, q))
    whole = pl.BlockSpec((LEN, WIDTH), lambda q, *_: (0, q))
    own = pl.BlockSpec((MODES, WIDTH), lambda q, *_: (0, 0))
    rows16 = pl.BlockSpec((1, MODES, WIDTH), lambda q, *_: (q, 0, 0))
    rows48 = pl.BlockSpec((1, 48, WIDTH), lambda q, *_: (q, 0, 0))
    residues = pl.BlockSpec((1, MODES, WIDTH), lambda q, *_: (q, 2, 0))
    rows32 = pl.BlockSpec((1, 32, WIDTH), lambda q, *_: (q, 0, 0))
    rows64 = pl.BlockSpec((1, 64, WIDTH), lambda q, *_: (q, 0, 0))
    table_f = pl.BlockSpec((2 * LEN, LEN), lambda q, *_: (0, 0))
    table_i = pl.BlockSpec((LEN, 2 * LEN), lambda q, *_: (0, 0))
    shape_part = jax.ShapeDtypeStruct((HALF, half), BF16)
    shape_whole = jax.ShapeDtypeStruct((LEN, half), BF16)
    shape_rows = jax.ShapeDtypeStruct((BLOCKS, 32, WIDTH), BF16)
    wide = pltpu.VMEM((LEN, WIDTH), F32)
    narrow = pltpu.VMEM((32, WIDTH), F32)

    pair = pl.BlockSpec((HALF, 4 * WIDTH), lambda q, *_: (0, q))
    pair_half = pl.BlockSpec((HALF, 2 * WIDTH), lambda q, *_: (0, q))
    x_keep, g_keep, x_give, g_give = call(
        gate_kernel, "gate", cost(2 * moved, 12 * moved), (BLOCKS // 2,), [pair] * 4, [pair_half] * 4, [shape_part] * 4, [],
        (core, keys2, values2, out_grad2, queries2),
    )
    x_give, g_give, prm = lax.optimization_barrier((x_give, g_give, prm))
    x_got, g_got, prm_got = swap(x_give), swap(g_give), swap(prm)
    x, g, sums, grad_a = call(
        state_kernel, "states", cost(7 * work, 8 * moved), (BLOCKS,), [rows16, own] + [part] * 4,
        [whole, whole, rows48, rows32],
        [shape_whole, shape_whole, jax.ShapeDtypeStruct((BLOCKS, 48, WIDTH), F32), shape_rows],
        [wide, wide, narrow], (core, prm, residue, x_keep, g_keep, x_got, g_got),
    )
    sums_own = exchange(sums)
    prm_got, x = lax.optimization_barrier((prm_got, x))
    grad_b = call(
        grad_kernel, "local_grads", cost(6 * work, 4 * moved), (BLOCKS,), [rows16, table_f, table_i, whole, whole],
        rows32, shape_rows, [wide, narrow], (prm, forward, inverse, x, g), False,
    )
    ends_own = pl.pallas_call(
        scan_kernel,
        out_shape=jax.ShapeDtypeStruct((BLOCKS, 128, WIDTH), BF16),
        compiler_params=params(),
        name="scan",
    )(sums_own, grad_a, grad_b, rate, residue)
    ends = exchange(ends_own)
    few = pltpu.VMEM((MODES, WIDTH), F32)
    conv_keep, back_keep, conv_give, back_give = call(
        local_kernel, "local_conv", cost(5 * work, 8 * moved), (BLOCKS,),
        [rows16, residues, table_f, table_i, whole, whole], [part] * 4, [shape_part] * 4, [wide] + [few] * 3,
        (core, prm, sums_own, forward, inverse, x, g),
    )
    conv_got, back_got = swap(conv_give), swap(back_give)
    ends, conv_keep = lax.optimization_barrier((ends, conv_keep))
    ends_got = swap(ends)
    owned = lambda rows, i=0: pl.BlockSpec((BLOCKS, rows, WIDTH), lambda *_: (0, i, 0))
    grads = call(
        owner_grad_kernel, "owner_grads", cost(1000, 2000000), (1,), [owned(32), owned(64, 1), own, own],
        pl.BlockSpec((8, 32, WIDTH), lambda *_: (0, 0, 0)), jax.ShapeDtypeStruct((8, 32, WIDTH), F32), [],
        (sums_own, ends, rate, residue), False,
    )
    grads, ends = lax.optimization_barrier((grads, ends))
    grads = lax.all_to_all(grads, "dp", split_axis=0, concat_axis=0, tiled=True)
    big = pl.BlockSpec((HALF, 2 * WIDTH), lambda q, *_: (0, q))
    pair_specs = [rows16, rows16, rows64, rows64]
    shape_out = jax.ShapeDtypeStruct((HALF, chans), BF16)
    half_wide = pltpu.VMEM((2, HALF, WIDTH), F32)
    few_two = pltpu.VMEM((2, MODES, WIDTH), F32)
    outs = call(
        finish_kernel, "finish", cost(4 * work, 20 * moved), (BLOCKS,),
        pair_specs + [part] * 4 + [big] * 3, [big] * 3, [shape_out] * 3,
        [few_two] * 4 + [half_wide] * 2,
        (core, prm, prm_got, ends, ends_got, conv_keep, back_keep, conv_got, back_got, out_grad2, keys2, values2),
    )
    outs, grads = lax.optimization_barrier((outs, grads))
    grads = jnp.sum(grads, 0)
    query_grad, key_grad, value_grad = (a.reshape(queries.shape) for a in outs)
    return query_grad, key_grad, value_grad, grads[:MODES], grads[MODES:]


def solution(mesh):
    wide = P("dp", "ctx", None)
    narrow = P(None, "ctx")
    return jax.shard_map(
        body,
        mesh=mesh,
        in_specs=(wide,) * 4 + (narrow,) * 2,
        out_specs=(wide,) * 3 + (narrow,) * 2,
        check_vma=False,
    )
```

```python
import math

import jax
import jax.numpy as jnp
import ml_dtypes
import numpy as np
from jax import lax
from jax.experimental import pallas as pl
from jax.experimental.pallas import tpu as pltpu
from jax.sharding import PartitionSpec as P

HALF = 128
LEN = 256
STEPS = LEN // 8
MODES = 16
WIDTH = 512
BLOCKS = 8
TOGETHER = 4
PART = 256
F32 = jnp.float32
BF16 = jnp.bfloat16


def tables():
    angle = math.pi * np.outer(2 * np.arange(LEN) + 1, np.arange(LEN)) / (2 * LEN)
    forward = np.concatenate([np.cos(angle), -np.sin(angle)], 0)
    inverse = forward.T / LEN
    return forward.astype(ml_dtypes.bfloat16), inverse.astype(ml_dtypes.bfloat16)


def params(vmem=64):
    return pltpu.CompilerParams(vmem_limit_bytes=vmem * 1024 * 1024)


def cost(ops, moved):
    return pl.CostEstimate(flops=ops, bytes_accessed=moved, transcendentals=0)


def product(left, right):
    return (left.astype(F32) * right.astype(F32)).astype(BF16)


def total(terms):
    terms = list(terms)
    while len(terms) > 1:
        terms = [u + v for u, v in zip(terms[::2], terms[1::2])]
    return terms[0]


def gate_kernel(core, keys, values, out_grad, queries, x_keep, g_keep, x_give, g_give):
    even = core[0] == 0
    for left, right, keep, give in ((keys, values, x_keep, x_give), (out_grad, queries, g_keep, g_give)):
        for q in range(keep.shape[1] // WIDTH):
            first = pl.ds(2 * q * WIDTH, WIDTH)
            second = pl.ds((2 * q + 1) * WIDTH, WIDTH)
            u = product(left[:, first], right[:, first])
            v = product(left[:, second], right[:, second])
            keep[:, pl.ds(q * WIDTH, WIDTH)] = jnp.where(even, u, v)
            give[:, pl.ds(q * WIDTH, WIDTH)] = jnp.where(even, v, u)


def ladder(width, flip=False):
    s = lax.broadcasted_iota(jnp.int32, (8, width), 0).astype(F32)
    return 7.0 - s if flip else s


def column(values):
    return jnp.sum(values, axis=0, keepdims=True)


def power_sums(rates, signals, lanes):
    y = [jnp.broadcast_to(jnp.exp(-8.0 * rate), (8, 128)) for rate in rates]
    power = list(y)

    def load(ref, back, k):
        return ref[pl.ds(LEN - 8 - 8 * k if back else 8 * k, 8), lanes]

    v = [[load(ref, back, 0)] * len(rates) for ref, back in signals]
    d = [list(u) for u in v]
    for k in range(1, STEPS):
        for i, (ref, back) in enumerate(signals):
            sk = load(ref, back, k)
            for j in range(len(rates)):
                v[i][j] = v[i][j] + power[j] * sk
                if k < STEPS - 1:
                    d[i][j] = d[i][j] + v[i][j]
        if k < STEPS - 1:
            power = [p * u for p, u in zip(power, y)]
    last = float(STEPS - 1)
    return [[(vj, last * vj - dj) for vj, dj in zip(vi, di)] for vi, di in zip(v, d)]


def state_kernel(prm, residue, x, g, sums, parts, x_s, g_s, sums_s):
    x_s[...] = x[...].astype(F32)
    g_s[...] = g[...].astype(F32)
    for tile in range(WIDTH // 128):
        lanes = pl.ds(128 * tile, 128)
        s, r = ladder(128), ladder(128, True)

        def some(group, carry):
            modes = [TOGETHER * group + i for i in range(TOGETHER)]
            rates = [prm[0, pl.ds(m, 1), lanes] for m in modes]
            xs = power_sums(rates, ((x_s, True), (g_s, False)), lanes)
            for m, rate, (v, d) in zip(modes, rates, xs[0]):
                weight = jnp.exp(-rate * r)
                sums[0, pl.ds(m, 1), lanes] = column(weight * v)
                sums_s[pl.ds(m, 1), lanes] = column(weight * (8.0 * d + r * v))
            for m, rate, (v, d) in zip(modes, rates, xs[1]):
                weight = jnp.exp(-rate * s)
                sums[0, pl.ds(MODES + m, 1), lanes] = column(weight * v)
                sums_s[pl.ds(MODES + m, 1), lanes] = column(weight * (8.0 * d + s * v))
            return carry

        lax.fori_loop(0, MODES // TOGETHER, some, 0, unroll=True)
    parts[0] = sums_s[...].astype(BF16)
    sums[0, 2 * MODES : 3 * MODES, :] = residue[...]


def dft(table, signal):
    return jnp.dot(table, signal, preferred_element_type=F32)


def correlate(forward, inverse, left, right):
    lr, li, rr, ri = left[:LEN], left[LEN:], right[:LEN], right[LEN:]
    both = jnp.concatenate([(lr * rr + li * ri).astype(BF16), (lr * ri - li * rr).astype(BF16)], 0)
    return dft(inverse, both)


def convolve(forward, inverse, left, right):
    lr, li, rr, ri = left[:LEN], left[LEN:], right[:LEN], right[LEN:]
    both = jnp.concatenate([(lr * rr - li * ri).astype(BF16), (lr * ri + li * rr).astype(BF16)], 0)
    return dft(inverse, both)


def lag_kernel(core, forward, inverse, x_keep, g_keep, x_got, g_got, x_out, g_out, lag):
    low = pl.multiple_of(core[0] * HALF, HALF)
    high = pl.multiple_of(HALF - core[0] * HALF, HALF)
    for keep, got, out in ((x_keep, x_got, x_out), (g_keep, g_got, g_out)):
        out[pl.ds(low, HALF), :] = keep[...]
        out[pl.ds(high, HALF), :] = got[...]
    fwd, inv = forward[...], inverse[...]
    lag[...] = correlate(fwd, inv, dft(fwd, x_out[...]), dft(fwd, g_out[...]))


def grad_kernel(prm, lag, grad_a, parts, sums_s):
    for tile in range(WIDTH // 128):
        lanes = pl.ds(128 * tile, 128)
        s = ladder(128)

        def some(group, carry):
            modes = [TOGETHER * group + i for i in range(TOGETHER)]
            rates = [prm[0, pl.ds(m, 1), lanes] for m in modes]
            (lags,) = power_sums(rates, ((lag, False),), lanes)
            for m, rate, (v, d) in zip(modes, rates, lags):
                weight = jnp.exp(-rate * s)
                sums_s[pl.ds(m, 1), lanes] = column(weight * v)
                sums_s[pl.ds(MODES + m, 1), lanes] = column(weight * (8.0 * d + s * v))
            return carry

        lax.fori_loop(0, MODES // TOGETHER, some, 0, unroll=True)
    parts[0, 0:32, :] = grad_a[0]
    parts[0, 32:64, :] = sums_s[...].astype(BF16)


def expand(minus, steps, heads, flip, put, count):
    for tile in range(WIDTH // 128):
        lanes = pl.ds(128 * tile, 128)
        s = ladder(128, flip)
        y = tuple(jnp.broadcast_to(steps[pl.ds(m, 1), lanes], (8, 128)) for m in range(MODES))
        z = tuple(heads[pl.ds(m, 1), lanes] * jnp.exp(minus[pl.ds(m, 1), lanes] * s) for m in range(MODES))
        for k in range(count):
            put(k, lanes, total(z))
            if k < count - 1:
                z = tuple(u * v for u, v in zip(z, y))


def local_kernel(core, prm, residue, forward, inverse, x, g, conv_keep, back_keep, conv_give, back_give, filt_s, minus_s, step_s, res_s):
    fwd, inv = forward[...], inverse[...]
    even = core[0] == 0
    minus_s[...] = -prm[0]
    step_s[...] = jnp.exp(-8.0 * prm[0])
    res_s[...] = residue[0]

    def put(k, lanes, rows):
        filt_s[pl.ds(8 * k, 8), lanes] = rows

    expand(minus_s, step_s, res_s, False, put, STEPS)
    for part in range(WIDTH // PART):
        lanes = pl.ds(PART * part, PART)
        filt = dft(fwd, filt_s[:, lanes].astype(BF16))
        conv = convolve(fwd, inv, filt, dft(fwd, x[:, lanes])).astype(BF16)
        back = correlate(fwd, inv, filt, dft(fwd, g[:, lanes])).astype(BF16)
        for both, keep, give in ((conv, conv_keep, conv_give), (back, back_keep, back_give)):
            keep[:, lanes] = jnp.where(even, both[:HALF], both[HALF:])
            give[:, lanes] = jnp.where(even, both[HALF:], both[:HALF])


def scan_kernel(sums, parts, own_rate, residue, out):
    rate = own_rate[...]
    scale = residue[...] * jnp.exp(-rate)
    far = jnp.exp(-float(LEN) * rate)

    def write(d, base, state):
        ends = scale * state
        near = ends.astype(BF16)
        out[d, base : base + MODES, :] = near
        out[d, base + MODES : base + 2 * MODES, :] = (ends - near.astype(F32)).astype(BF16)

    state = jnp.zeros((MODES, WIDTH), F32)
    for d in range(BLOCKS):
        write(d, 0, state)
        state = far * state + sums[d, 0:MODES, :]
    state = jnp.zeros((MODES, WIDTH), F32)
    for d in range(BLOCKS - 1, -1, -1):
        write(d, 2 * MODES, state)
        state = far * state + sums[d, MODES : 2 * MODES, :]


def owner_grad_kernel(sums, got, own_rate, residue, out):
    rate = own_rate[...]
    lam = jnp.exp(-rate)
    far = jnp.exp(-float(LEN) * rate)
    zero = jnp.zeros((MODES, WIDTH), F32)
    h, q, hg, pg, hb, qb = zero, zero, zero, zero, zero, zero
    for d in range(BLOCKS):
        b = sums[d, MODES : 2 * MODES, :]
        p, w, hd, pd = (got[d, 16 * i : 16 * i + 16, :].astype(F32) for i in range(4))
        hg = hg + hd
        pg = pg + pd
        hb = hb + h * b
        qb = qb + h * (w + b) + q * b
        q = far * (q + float(LEN) * h) + p
        h = far * h + sums[d, 0:MODES, :]
    first = hg + lam * hb
    second = -residue[...] * (pg + lam * qb)
    for b in range(out.shape[0]):
        out[b, 0:MODES, :] = first
        out[b, MODES : 2 * MODES, :] = second


def finish_kernel(
    core, prm, prm_got, ends, ends_got, conv_keep, back_keep, conv_got, back_got, out_grad, keys, values,
    query_out, key_out, value_out, minus_s, step_s, head_s, tail_s, conv_s, back_s,
):
    upper = core[0].astype(F32) * float(HALF)
    for h in range(2):
        mine = core[0] == h
        minus = -jnp.where(mine, prm[0], prm_got[0])
        edge = jnp.where(mine, ends[0], ends_got[0]).astype(F32)
        minus_s[h] = minus
        step_s[h] = jnp.exp(8.0 * minus)
        head_s[h] = (edge[0:16] + edge[16:32]) * jnp.exp(minus * upper)
        tail_s[h] = (edge[32:48] + edge[48:64]) * jnp.exp(minus * (float(HALF) - upper))

        def put_conv(k, lanes, rows):
            conv_s[h, pl.ds(8 * k, 8), lanes] = rows

        def put_back(k, lanes, rows):
            back_s[h, pl.ds(HALF - 8 - 8 * k, 8), lanes] = rows

        expand(minus_s.at[h], step_s.at[h], head_s.at[h], False, put_conv, HALF // 8)
        expand(minus_s.at[h], step_s.at[h], tail_s.at[h], True, put_back, HALF // 8)
        c = (jnp.where(mine, conv_keep[...], conv_got[...]).astype(F32) + conv_s[h]).astype(BF16)
        b = (jnp.where(mine, back_keep[...], back_got[...]).astype(F32) + back_s[h]).astype(BF16)
        lanes = pl.ds(h * WIDTH, WIDTH)
        query_out[:, lanes] = product(out_grad[:, lanes], c)
        key_out[:, lanes] = product(b, values[:, lanes])
        value_out[:, lanes] = product(b, keys[:, lanes])


def call(kernel, name, work, grid, in_specs, out_specs, shapes, scratch, operands, prefetch=True, aliases=None):
    spec = pltpu.PrefetchScalarGridSpec(
        num_scalar_prefetch=1 if prefetch else 0, grid=grid, in_specs=in_specs, out_specs=out_specs, scratch_shapes=scratch
    )
    return pl.pallas_call(
        kernel, grid_spec=spec, out_shape=shapes, compiler_params=params(), cost_estimate=work, name=name,
        input_output_aliases=aliases or {},
    )(*operands)


def swap(array):
    return lax.ppermute(array, "ctx", [(i, i ^ 1) for i in range(2 * BLOCKS)])


def exchange(array):
    groups = [[2 * q + c for q in range(BLOCKS)] for c in range(2)]
    return lax.all_to_all(array, "ctx", split_axis=0, concat_axis=0, axis_index_groups=groups, tiled=True)


def body(queries, keys, values, out_grad, residue, rate):
    chans = queries.shape[2]
    half = chans // 2
    queries2, keys2, values2, out_grad2 = (a.reshape(HALF, chans) for a in (queries, keys, values, out_grad))
    core = (lax.axis_index("ctx") % 2).astype(jnp.int32).reshape(1)
    forward, inverse = tables()
    owned = lambda rows, i=0: pl.BlockSpec((BLOCKS, rows, WIDTH), lambda *_: (0, i, 0))
    shape_payload = jax.ShapeDtypeStruct((BLOCKS, 128, WIDTH), BF16)
    work = LEN * half * MODES
    moved = LEN * half

    part = pl.BlockSpec((HALF, WIDTH), lambda q, *_: (0, q))
    whole = pl.BlockSpec((LEN, WIDTH), lambda q, *_: (0, q))
    own = pl.BlockSpec((MODES, WIDTH), lambda q, *_: (0, 0))
    rows16 = pl.BlockSpec((1, MODES, WIDTH), lambda q, *_: (q, 0, 0))
    rows48 = pl.BlockSpec((1, 48, WIDTH), lambda q, *_: (q, 0, 0))
    residues = pl.BlockSpec((1, MODES, WIDTH), lambda q, *_: (q, 2, 0))
    rows32 = pl.BlockSpec((1, 32, WIDTH), lambda q, *_: (q, 0, 0))
    rows64 = pl.BlockSpec((1, 64, WIDTH), lambda q, *_: (q, 0, 0))
    table_f = pl.BlockSpec((2 * LEN, LEN), lambda q, *_: (0, 0))
    table_i = pl.BlockSpec((LEN, 2 * LEN), lambda q, *_: (0, 0))
    shape_part = jax.ShapeDtypeStruct((HALF, half), BF16)
    shape_whole = jax.ShapeDtypeStruct((LEN, half), BF16)
    shape_rows = jax.ShapeDtypeStruct((BLOCKS, 32, WIDTH), BF16)
    wide = pltpu.VMEM((LEN, WIDTH), F32)
    narrow = pltpu.VMEM((32, WIDTH), F32)

    pair = pl.BlockSpec((HALF, 4 * WIDTH), lambda q, *_: (0, q))
    pair_half = pl.BlockSpec((HALF, 2 * WIDTH), lambda q, *_: (0, q))
    x_keep, g_keep, x_give, g_give = call(
        gate_kernel, "gate", cost(2 * moved, 12 * moved), (BLOCKS // 2,), [pair] * 4, [pair_half] * 4, [shape_part] * 4, [],
        (core, keys2, values2, out_grad2, queries2),
    )
    rates, x_give = lax.optimization_barrier((jnp.broadcast_to(rate[None], (BLOCKS, MODES, WIDTH)), x_give))
    prm = exchange(rates)
    x_got, g_got = swap(x_give), swap(g_give)
    double = pl.BlockSpec((HALF, 2 * WIDTH), lambda q, *_: (0, q))
    double_whole = pl.BlockSpec((LEN, 2 * WIDTH), lambda q, *_: (0, q))
    x, g, lag = call(
        lag_kernel, "lags", cost(work, 16 * moved), (BLOCKS // 2,), [table_f, table_i] + [double] * 4,
        [double_whole] * 3, [shape_whole, shape_whole, jax.ShapeDtypeStruct((LEN, half), F32)], [],
        (core, forward, inverse, x_keep, g_keep, x_got, g_got),
    )
    prm_got = swap(prm)
    sums, grad_a = call(
        state_kernel, "states", cost(7 * work, 4 * moved), (BLOCKS,), [rows16, own, whole, whole], [rows48, rows32],
        [jax.ShapeDtypeStruct((BLOCKS, 48, WIDTH), F32), shape_rows], [wide, wide, narrow], (prm, residue, x, g), False,
    )
    sums_own = exchange(sums)
    parts = call(
        grad_kernel, "local_grads", cost(4 * work, 4 * moved), (BLOCKS,), [rows16, whole, rows32],
        pl.BlockSpec((1, 64, WIDTH), lambda q, *_: (q, 1, 0)), shape_payload, [narrow], (prm, lag, grad_a), False,
    )
    prm_got, parts = lax.optimization_barrier((prm_got, parts))
    ends_own = call(
        scan_kernel, "scan", cost(1000, 1000000), (1,), [owned(32), pl.BlockSpec(memory_space=pl.ANY), own, own], owned(64),
        shape_payload, [], (sums_own, parts, rate, residue), False, {1: 0},
    )
    ends = exchange(ends_own)
    few = pltpu.VMEM((MODES, WIDTH), F32)
    conv_keep, back_keep, conv_give, back_give = call(
        local_kernel, "local_conv", cost(5 * work, 8 * moved), (BLOCKS,),
        [rows16, residues, table_f, table_i, whole, whole], [part] * 4, [shape_part] * 4, [wide] + [few] * 3,
        (core, prm, sums_own, forward, inverse, x, g),
    )
    conv_got, back_got = swap(conv_give), swap(back_give)
    ends, conv_keep = lax.optimization_barrier((ends, conv_keep))
    ends_got = swap(ends)
    grads = call(
        owner_grad_kernel, "owner_grads", cost(1000, 2000000), (1,), [owned(32), owned(64, 1), own, own],
        pl.BlockSpec((8, 32, WIDTH), lambda *_: (0, 0, 0)), jax.ShapeDtypeStruct((8, 32, WIDTH), F32), [],
        (sums_own, ends, rate, residue), False,
    )
    grads, ends = lax.optimization_barrier((grads, ends))
    grads = lax.all_to_all(grads, "dp", split_axis=0, concat_axis=0, tiled=True)
    big = pl.BlockSpec((HALF, 2 * WIDTH), lambda q, *_: (0, q))
    pair_specs = [rows16, rows16, rows64, rows64]
    shape_out = jax.ShapeDtypeStruct((HALF, chans), BF16)
    half_wide = pltpu.VMEM((2, HALF, WIDTH), F32)
    few_two = pltpu.VMEM((2, MODES, WIDTH), F32)
    outs = call(
        finish_kernel, "finish", cost(4 * work, 20 * moved), (BLOCKS,),
        pair_specs + [part] * 4 + [big] * 3, [big] * 3, [shape_out] * 3,
        [few_two] * 4 + [half_wide] * 2,
        (core, prm, prm_got, ends, ends_got, conv_keep, back_keep, conv_got, back_got, out_grad2, keys2, values2),
    )
    outs, grads = lax.optimization_barrier((outs, grads))
    grads = jnp.sum(grads, 0)
    query_grad, key_grad, value_grad = (a.reshape(queries.shape) for a in outs)
    return query_grad, key_grad, value_grad, grads[:MODES], grads[MODES:]


def solution(mesh):
    wide = P("dp", "ctx", None)
    narrow = P(None, "ctx")
    return jax.shard_map(
        body,
        mesh=mesh,
        in_specs=(wide,) * 4 + (narrow,) * 2,
        out_specs=(wide,) * 3 + (narrow,) * 2,
        check_vma=False,
    )
```

```python
import math

import jax
import jax.numpy as jnp
import ml_dtypes
import numpy as np
from jax import lax
from jax.experimental import pallas as pl
from jax.experimental.pallas import tpu as pltpu
from jax.sharding import PartitionSpec as P

HALF = 128
LEN = 256
STEPS = LEN // 8
MODES = 16
WIDTH = 512
BLOCKS = 8
TOGETHER = 4
PART = 256
F32 = jnp.float32
BF16 = jnp.bfloat16


def tables():
    angle = math.pi * np.outer(2 * np.arange(LEN) + 1, np.arange(LEN)) / (2 * LEN)
    forward = np.concatenate([np.cos(angle), -np.sin(angle)], 0)
    inverse = forward.T / LEN
    return forward.astype(ml_dtypes.bfloat16), inverse.astype(ml_dtypes.bfloat16)


def params(vmem=64):
    return pltpu.CompilerParams(vmem_limit_bytes=vmem * 1024 * 1024)


def cost(ops, moved):
    return pl.CostEstimate(flops=ops, bytes_accessed=moved, transcendentals=0)


def product(left, right):
    return (left.astype(F32) * right.astype(F32)).astype(BF16)


def total(terms):
    terms = list(terms)
    while len(terms) > 1:
        terms = [u + v for u, v in zip(terms[::2], terms[1::2])]
    return terms[0]


def gate_kernel(core, rate, keys, values, out_grad, queries, copies, x_keep, g_keep, x_give, g_give):
    even = core[0] == 0

    @pl.when(pl.program_id(0) == 0)
    def _():
        for q in range(BLOCKS):
            copies[q] = rate[...]

    for left, right, keep, give in ((keys, values, x_keep, x_give), (out_grad, queries, g_keep, g_give)):
        for q in range(keep.shape[1] // WIDTH):
            first = pl.ds(2 * q * WIDTH, WIDTH)
            second = pl.ds((2 * q + 1) * WIDTH, WIDTH)
            u = product(left[:, first], right[:, first])
            v = product(left[:, second], right[:, second])
            keep[:, pl.ds(q * WIDTH, WIDTH)] = jnp.where(even, u, v)
            give[:, pl.ds(q * WIDTH, WIDTH)] = jnp.where(even, v, u)


def ladder(width, flip=False):
    s = lax.broadcasted_iota(jnp.int32, (8, width), 0).astype(F32)
    return 7.0 - s if flip else s


def column(values):
    return jnp.sum(values, axis=0, keepdims=True)


def power_sums(rates, signals, lanes):
    y = [jnp.broadcast_to(jnp.exp(-8.0 * rate), (8, 128)) for rate in rates]
    power = list(y)

    def load(ref, back, k):
        return ref[pl.ds(LEN - 8 - 8 * k if back else 8 * k, 8), lanes]

    v = [[load(ref, back, 0)] * len(rates) for ref, back in signals]
    d = [list(u) for u in v]
    for k in range(1, STEPS):
        for i, (ref, back) in enumerate(signals):
            sk = load(ref, back, k)
            for j in range(len(rates)):
                v[i][j] = v[i][j] + power[j] * sk
                if k < STEPS - 1:
                    d[i][j] = d[i][j] + v[i][j]
        if k < STEPS - 1:
            power = [p * u for p, u in zip(power, y)]
    last = float(STEPS - 1)
    return [[(vj, last * vj - dj) for vj, dj in zip(vi, di)] for vi, di in zip(v, d)]


def state_kernel(prm, residue, x, g, sums, parts, x_s, g_s, sums_s):
    x_s[...] = x[...].astype(F32)
    g_s[...] = g[...].astype(F32)
    for tile in range(WIDTH // 128):
        lanes = pl.ds(128 * tile, 128)
        s, r = ladder(128), ladder(128, True)

        def some(group, carry):
            modes = [TOGETHER * group + i for i in range(TOGETHER)]
            rates = [prm[0, pl.ds(m, 1), lanes] for m in modes]
            xs = power_sums(rates, ((x_s, True), (g_s, False)), lanes)
            for m, rate, (v, d) in zip(modes, rates, xs[0]):
                weight = jnp.exp(-rate * r)
                sums[0, pl.ds(m, 1), lanes] = column(weight * v)
                sums_s[pl.ds(m, 1), lanes] = column(weight * (8.0 * d + r * v))
            for m, rate, (v, d) in zip(modes, rates, xs[1]):
                weight = jnp.exp(-rate * s)
                sums[0, pl.ds(MODES + m, 1), lanes] = column(weight * v)
                sums_s[pl.ds(MODES + m, 1), lanes] = column(weight * (8.0 * d + s * v))
            return carry

        lax.fori_loop(0, MODES // TOGETHER, some, 0, unroll=True)
    parts[0] = sums_s[...].astype(BF16)
    sums[0, 2 * MODES : 3 * MODES, :] = residue[...]


def dft(table, signal):
    return jnp.dot(table, signal, preferred_element_type=F32)


def correlate(forward, inverse, left, right):
    lr, li, rr, ri = left[:LEN], left[LEN:], right[:LEN], right[LEN:]
    both = jnp.concatenate([(lr * rr + li * ri).astype(BF16), (lr * ri - li * rr).astype(BF16)], 0)
    return dft(inverse, both)


def convolve(forward, inverse, left, right):
    lr, li, rr, ri = left[:LEN], left[LEN:], right[:LEN], right[LEN:]
    both = jnp.concatenate([(lr * rr - li * ri).astype(BF16), (lr * ri + li * rr).astype(BF16)], 0)
    return dft(inverse, both)


def lag_kernel(core, forward, inverse, x_keep, g_keep, x_got, g_got, x_out, g_out, lag):
    low = pl.multiple_of(core[0] * HALF, HALF)
    high = pl.multiple_of(HALF - core[0] * HALF, HALF)
    for keep, got, out in ((x_keep, x_got, x_out), (g_keep, g_got, g_out)):
        out[pl.ds(low, HALF), :] = keep[...]
        out[pl.ds(high, HALF), :] = got[...]
    fwd, inv = forward[...], inverse[...]
    lag[...] = correlate(fwd, inv, dft(fwd, x_out[...]), dft(fwd, g_out[...]))


def grad_kernel(prm, lag, grad_a, parts, sums_s):
    for tile in range(WIDTH // 128):
        lanes = pl.ds(128 * tile, 128)
        s = ladder(128)

        def some(group, carry):
            modes = [TOGETHER * group + i for i in range(TOGETHER)]
            rates = [prm[0, pl.ds(m, 1), lanes] for m in modes]
            (lags,) = power_sums(rates, ((lag, False),), lanes)
            for m, rate, (v, d) in zip(modes, rates, lags):
                weight = jnp.exp(-rate * s)
                sums_s[pl.ds(m, 1), lanes] = column(weight * v)
                sums_s[pl.ds(MODES + m, 1), lanes] = column(weight * (8.0 * d + s * v))
            return carry

        lax.fori_loop(0, MODES // TOGETHER, some, 0, unroll=True)
    parts[0, 0:32, :] = grad_a[0]
    parts[0, 32:64, :] = sums_s[...].astype(BF16)


def expand(minus, steps, heads, flip, put, count):
    for tile in range(WIDTH // 128):
        lanes = pl.ds(128 * tile, 128)
        s = ladder(128, flip)
        y = tuple(jnp.broadcast_to(steps[pl.ds(m, 1), lanes], (8, 128)) for m in range(MODES))
        z = tuple(heads[pl.ds(m, 1), lanes] * jnp.exp(minus[pl.ds(m, 1), lanes] * s) for m in range(MODES))
        for k in range(count):
            put(k, lanes, total(z))
            if k < count - 1:
                z = tuple(u * v for u, v in zip(z, y))


def local_kernel(core, prm, residue, forward, inverse, x, g, conv_keep, back_keep, conv_give, back_give, filt_s, minus_s, step_s, res_s):
    fwd, inv = forward[...], inverse[...]
    even = core[0] == 0
    minus_s[...] = -prm[0]
    step_s[...] = jnp.exp(-8.0 * prm[0])
    res_s[...] = residue[0]

    def put(k, lanes, rows):
        filt_s[pl.ds(8 * k, 8), lanes] = rows

    expand(minus_s, step_s, res_s, False, put, STEPS)
    for part in range(WIDTH // PART):
        lanes = pl.ds(PART * part, PART)
        filt = dft(fwd, filt_s[:, lanes].astype(BF16))
        conv = convolve(fwd, inv, filt, dft(fwd, x[:, lanes])).astype(BF16)
        back = correlate(fwd, inv, filt, dft(fwd, g[:, lanes])).astype(BF16)
        for both, keep, give in ((conv, conv_keep, conv_give), (back, back_keep, back_give)):
            keep[:, lanes] = jnp.where(even, both[:HALF], both[HALF:])
            give[:, lanes] = jnp.where(even, both[HALF:], both[:HALF])


def scan_kernel(sums, parts, own_rate, residue, out):
    rate = own_rate[...]
    scale = residue[...] * jnp.exp(-rate)
    far = jnp.exp(-float(LEN) * rate)

    def write(d, base, state):
        ends = scale * state
        near = ends.astype(BF16)
        out[d, base : base + MODES, :] = near
        out[d, base + MODES : base + 2 * MODES, :] = (ends - near.astype(F32)).astype(BF16)

    state = jnp.zeros((MODES, WIDTH), F32)
    for d in range(BLOCKS):
        write(d, 0, state)
        state = far * state + sums[d, 0:MODES, :]
    state = jnp.zeros((MODES, WIDTH), F32)
    for d in range(BLOCKS - 1, -1, -1):
        write(d, 2 * MODES, state)
        state = far * state + sums[d, MODES : 2 * MODES, :]


def owner_grad_kernel(sums, got, own_rate, residue, out):
    rate = own_rate[...]
    lam = jnp.exp(-rate)
    far = jnp.exp(-float(LEN) * rate)
    zero = jnp.zeros((MODES, WIDTH), F32)
    h, q, hg, pg, hb, qb = zero, zero, zero, zero, zero, zero
    for d in range(BLOCKS):
        b = sums[d, MODES : 2 * MODES, :]
        p, w, hd, pd = (got[d, 16 * i : 16 * i + 16, :].astype(F32) for i in range(4))
        hg = hg + hd
        pg = pg + pd
        hb = hb + h * b
        qb = qb + h * (w + b) + q * b
        q = far * (q + float(LEN) * h) + p
        h = far * h + sums[d, 0:MODES, :]
    first = hg + lam * hb
    second = -residue[...] * (pg + lam * qb)
    for b in range(out.shape[0]):
        out[b, 0:MODES, :] = first
        out[b, MODES : 2 * MODES, :] = second


def sum_kernel(grads, residue_grad, rate_grad):
    residue_grad[...] = total(grads[b, 0:MODES, :] for b in range(grads.shape[0]))
    rate_grad[...] = total(grads[b, MODES : 2 * MODES, :] for b in range(grads.shape[0]))


def finish_kernel(
    core, prm, prm_got, ends, ends_got, conv_keep, back_keep, conv_got, back_got, out_grad, keys, values,
    query_out, key_out, value_out, minus_s, step_s, head_s, tail_s, conv_s, back_s,
):
    upper = core[0].astype(F32) * float(HALF)
    for h in range(2):
        mine = core[0] == h
        minus = -jnp.where(mine, prm[0], prm_got[0])
        edge = jnp.where(mine, ends[0], ends_got[0]).astype(F32)
        minus_s[h] = minus
        step_s[h] = jnp.exp(8.0 * minus)
        head_s[h] = (edge[0:16] + edge[16:32]) * jnp.exp(minus * upper)
        tail_s[h] = (edge[32:48] + edge[48:64]) * jnp.exp(minus * (float(HALF) - upper))

        def put_conv(k, lanes, rows):
            conv_s[h, pl.ds(8 * k, 8), lanes] = rows

        def put_back(k, lanes, rows):
            back_s[h, pl.ds(HALF - 8 - 8 * k, 8), lanes] = rows

        expand(minus_s.at[h], step_s.at[h], head_s.at[h], False, put_conv, HALF // 8)
        expand(minus_s.at[h], step_s.at[h], tail_s.at[h], True, put_back, HALF // 8)
        c = (jnp.where(mine, conv_keep[...], conv_got[...]).astype(F32) + conv_s[h]).astype(BF16)
        b = (jnp.where(mine, back_keep[...], back_got[...]).astype(F32) + back_s[h]).astype(BF16)
        lanes = pl.ds(h * WIDTH, WIDTH)
        query_out[:, lanes] = product(out_grad[:, lanes], c)
        key_out[:, lanes] = product(b, values[:, lanes])
        value_out[:, lanes] = product(b, keys[:, lanes])


def call(kernel, name, work, grid, in_specs, out_specs, shapes, scratch, operands, prefetch=True, aliases=None):
    spec = pltpu.PrefetchScalarGridSpec(
        num_scalar_prefetch=1 if prefetch else 0, grid=grid, in_specs=in_specs, out_specs=out_specs, scratch_shapes=scratch
    )
    return pl.pallas_call(
        kernel, grid_spec=spec, out_shape=shapes, compiler_params=params(), cost_estimate=work, name=name,
        input_output_aliases=aliases or {},
    )(*operands)


def swap(array):
    return lax.ppermute(array, "ctx", [(i, i ^ 1) for i in range(2 * BLOCKS)])


def exchange(array):
    groups = [[2 * q + c for q in range(BLOCKS)] for c in range(2)]
    return lax.all_to_all(array, "ctx", split_axis=0, concat_axis=0, axis_index_groups=groups, tiled=True)


def body(queries, keys, values, out_grad, residue, rate):
    chans = queries.shape[2]
    half = chans // 2
    queries2, keys2, values2, out_grad2 = (a.reshape(HALF, chans) for a in (queries, keys, values, out_grad))
    core = (lax.axis_index("ctx") % 2).astype(jnp.int32).reshape(1)
    forward, inverse = tables()
    owned = lambda rows, i=0: pl.BlockSpec((BLOCKS, rows, WIDTH), lambda *_: (0, i, 0))
    shape_payload = jax.ShapeDtypeStruct((BLOCKS, 128, WIDTH), BF16)
    work = LEN * half * MODES
    moved = LEN * half

    part = pl.BlockSpec((HALF, WIDTH), lambda q, *_: (0, q))
    whole = pl.BlockSpec((LEN, WIDTH), lambda q, *_: (0, q))
    own = pl.BlockSpec((MODES, WIDTH), lambda q, *_: (0, 0))
    rows16 = pl.BlockSpec((1, MODES, WIDTH), lambda q, *_: (q, 0, 0))
    rows48 = pl.BlockSpec((1, 48, WIDTH), lambda q, *_: (q, 0, 0))
    residues = pl.BlockSpec((1, MODES, WIDTH), lambda q, *_: (q, 2, 0))
    rows32 = pl.BlockSpec((1, 32, WIDTH), lambda q, *_: (q, 0, 0))
    rows64 = pl.BlockSpec((1, 64, WIDTH), lambda q, *_: (q, 0, 0))
    table_f = pl.BlockSpec((2 * LEN, LEN), lambda q, *_: (0, 0))
    table_i = pl.BlockSpec((LEN, 2 * LEN), lambda q, *_: (0, 0))
    shape_part = jax.ShapeDtypeStruct((HALF, half), BF16)
    shape_whole = jax.ShapeDtypeStruct((LEN, half), BF16)
    shape_rows = jax.ShapeDtypeStruct((BLOCKS, 32, WIDTH), BF16)
    wide = pltpu.VMEM((LEN, WIDTH), F32)
    narrow = pltpu.VMEM((32, WIDTH), F32)

    pair = pl.BlockSpec((HALF, 4 * WIDTH), lambda q, *_: (0, q))
    pair_half = pl.BlockSpec((HALF, 2 * WIDTH), lambda q, *_: (0, q))
    copies, x_keep, g_keep, x_give, g_give = call(
        gate_kernel, "gate", cost(2 * moved, 12 * moved), (BLOCKS // 2,), [own] + [pair] * 4,
        [pl.BlockSpec((BLOCKS, MODES, WIDTH), lambda *_: (0, 0, 0))] + [pair_half] * 4,
        [jax.ShapeDtypeStruct((BLOCKS, MODES, WIDTH), F32)] + [shape_part] * 4, [],
        (core, rate, keys2, values2, out_grad2, queries2),
    )
    prm = exchange(copies)
    x_got, g_got = swap(x_give), swap(g_give)
    double = pl.BlockSpec((HALF, 2 * WIDTH), lambda q, *_: (0, q))
    double_whole = pl.BlockSpec((LEN, 2 * WIDTH), lambda q, *_: (0, q))
    x, g, lag = call(
        lag_kernel, "lags", cost(work, 16 * moved), (BLOCKS // 2,), [table_f, table_i] + [double] * 4,
        [double_whole] * 3, [shape_whole, shape_whole, jax.ShapeDtypeStruct((LEN, half), F32)], [],
        (core, forward, inverse, x_keep, g_keep, x_got, g_got),
    )
    prm_got = swap(prm)
    sums, grad_a = call(
        state_kernel, "states", cost(7 * work, 4 * moved), (BLOCKS,), [rows16, own, whole, whole], [rows48, rows32],
        [jax.ShapeDtypeStruct((BLOCKS, 48, WIDTH), F32), shape_rows], [wide, wide, narrow], (prm, residue, x, g), False,
    )
    sums_own = exchange(sums)
    parts = call(
        grad_kernel, "local_grads", cost(4 * work, 4 * moved), (BLOCKS,), [rows16, whole, rows32],
        pl.BlockSpec((1, 64, WIDTH), lambda q, *_: (q, 1, 0)), shape_payload, [narrow], (prm, lag, grad_a), False,
    )
    prm_got, parts = lax.optimization_barrier((prm_got, parts))
    ends_own = call(
        scan_kernel, "scan", cost(1000, 1000000), (1,), [owned(32), pl.BlockSpec(memory_space=pl.ANY), own, own], owned(64),
        shape_payload, [], (sums_own, parts, rate, residue), False, {1: 0},
    )
    ends = exchange(ends_own)
    few = pltpu.VMEM((MODES, WIDTH), F32)
    conv_keep, back_keep, conv_give, back_give = call(
        local_kernel, "local_conv", cost(5 * work, 8 * moved), (BLOCKS,),
        [rows16, residues, table_f, table_i, whole, whole], [part] * 4, [shape_part] * 4, [wide] + [few] * 3,
        (core, prm, sums_own, forward, inverse, x, g),
    )
    conv_got, back_got = swap(conv_give), swap(back_give)
    ends, conv_keep = lax.optimization_barrier((ends, conv_keep))
    ends_got = swap(ends)
    grads = call(
        owner_grad_kernel, "owner_grads", cost(1000, 2000000), (1,), [owned(32), owned(64, 1), own, own],
        pl.BlockSpec((8, 32, WIDTH), lambda *_: (0, 0, 0)), jax.ShapeDtypeStruct((8, 32, WIDTH), F32), [],
        (sums_own, ends, rate, residue), False,
    )
    grads, ends = lax.optimization_barrier((grads, ends))
    grads = lax.all_to_all(grads, "dp", split_axis=0, concat_axis=0, tiled=True)
    big = pl.BlockSpec((HALF, 2 * WIDTH), lambda q, *_: (0, q))
    pair_specs = [rows16, rows16, rows64, rows64]
    shape_out = jax.ShapeDtypeStruct((HALF, chans), BF16)
    half_wide = pltpu.VMEM((2, HALF, WIDTH), F32)
    few_two = pltpu.VMEM((2, MODES, WIDTH), F32)
    outs = call(
        finish_kernel, "finish", cost(4 * work, 20 * moved), (BLOCKS,),
        pair_specs + [part] * 4 + [big] * 3, [big] * 3, [shape_out] * 3,
        [few_two] * 4 + [half_wide] * 2,
        (core, prm, prm_got, ends, ends_got, conv_keep, back_keep, conv_got, back_got, out_grad2, keys2, values2),
    )
    outs, grads = lax.optimization_barrier((outs, grads))
    residue_grad, rate_grad = pl.pallas_call(
        sum_kernel,
        out_shape=[jax.ShapeDtypeStruct((MODES, WIDTH), F32)] * 2,
        compiler_params=params(),
        name="sum_grads",
    )(grads)
    query_grad, key_grad, value_grad = (a.reshape(queries.shape) for a in outs)
    return query_grad, key_grad, value_grad, residue_grad, rate_grad


def solution(mesh):
    wide = P("dp", "ctx", None)
    narrow = P(None, "ctx")
    return jax.shard_map(
        body,
        mesh=mesh,
        in_specs=(wide,) * 4 + (narrow,) * 2,
        out_specs=(wide,) * 3 + (narrow,) * 2,
        check_vma=False,
    )
```

```python
import math

import jax
import jax.numpy as jnp
import ml_dtypes
import numpy as np
from jax import lax
from jax.experimental import pallas as pl
from jax.experimental.pallas import tpu as pltpu
from jax.sharding import PartitionSpec as P

HALF = 128
LEN = 256
STEPS = LEN // 8
MODES = 16
WIDTH = 512
BLOCKS = 8
TOGETHER = 4
PART = 256
F32 = jnp.float32
BF16 = jnp.bfloat16


def tables():
    angle = math.pi * np.outer(2 * np.arange(LEN) + 1, np.arange(LEN)) / (2 * LEN)
    forward = np.concatenate([np.cos(angle), -np.sin(angle)], 0)
    inverse = forward.T / LEN
    return forward.astype(ml_dtypes.bfloat16), inverse.astype(ml_dtypes.bfloat16)


def params(vmem=64):
    return pltpu.CompilerParams(vmem_limit_bytes=vmem * 1024 * 1024)


def cost(ops, moved):
    return pl.CostEstimate(flops=ops, bytes_accessed=moved, transcendentals=0)


def product(left, right):
    return (left.astype(F32) * right.astype(F32)).astype(BF16)


def total(terms):
    terms = list(terms)
    while len(terms) > 1:
        terms = [u + v for u, v in zip(terms[::2], terms[1::2])]
    return terms[0]


def gate_kernel(core, rate, keys, values, out_grad, queries, copies, x_keep, g_keep, x_give, g_give):
    even = core[0] == 0

    @pl.when(pl.program_id(0) == 0)
    def _():
        for q in range(BLOCKS):
            copies[q] = rate[...]

    for left, right, keep, give in ((keys, values, x_keep, x_give), (out_grad, queries, g_keep, g_give)):
        for q in range(keep.shape[1] // WIDTH):
            first = pl.ds(2 * q * WIDTH, WIDTH)
            second = pl.ds((2 * q + 1) * WIDTH, WIDTH)
            u = product(left[:, first], right[:, first])
            v = product(left[:, second], right[:, second])
            keep[:, pl.ds(q * WIDTH, WIDTH)] = jnp.where(even, u, v)
            give[:, pl.ds(q * WIDTH, WIDTH)] = jnp.where(even, v, u)


def ladder(width, flip=False):
    s = lax.broadcasted_iota(jnp.int32, (8, width), 0).astype(F32)
    return 7.0 - s if flip else s


def column(values):
    return jnp.sum(values, axis=0, keepdims=True)


def power_sums(rates, signals, lanes):
    y = [jnp.broadcast_to(jnp.exp(-8.0 * rate), (8, 128)) for rate in rates]
    power = list(y)

    def load(ref, back, k):
        return ref[pl.ds(LEN - 8 - 8 * k if back else 8 * k, 8), lanes]

    v = [[load(ref, back, 0)] * len(rates) for ref, back in signals]
    d = [list(u) for u in v]
    for k in range(1, STEPS):
        for i, (ref, back) in enumerate(signals):
            sk = load(ref, back, k)
            for j in range(len(rates)):
                v[i][j] = v[i][j] + power[j] * sk
                if k < STEPS - 1:
                    d[i][j] = d[i][j] + v[i][j]
        if k < STEPS - 1:
            power = [p * u for p, u in zip(power, y)]
    last = float(STEPS - 1)
    return [[(vj, last * vj - dj) for vj, dj in zip(vi, di)] for vi, di in zip(v, d)]


def state_kernel(prm, residue, x, g, sums, parts, x_s, g_s, sums_s):
    x_s[...] = x[...].astype(F32)
    g_s[...] = g[...].astype(F32)
    for tile in range(WIDTH // 128):
        lanes = pl.ds(128 * tile, 128)
        s, r = ladder(128), ladder(128, True)

        def some(group, carry):
            modes = [TOGETHER * group + i for i in range(TOGETHER)]
            rates = [prm[0, pl.ds(m, 1), lanes] for m in modes]
            xs = power_sums(rates, ((x_s, True), (g_s, False)), lanes)
            for m, rate, (v, d) in zip(modes, rates, xs[0]):
                weight = jnp.exp(-rate * r)
                sums[0, pl.ds(m, 1), lanes] = column(weight * v)
                sums_s[pl.ds(m, 1), lanes] = column(weight * (8.0 * d + r * v))
            for m, rate, (v, d) in zip(modes, rates, xs[1]):
                weight = jnp.exp(-rate * s)
                sums[0, pl.ds(MODES + m, 1), lanes] = column(weight * v)
                sums_s[pl.ds(MODES + m, 1), lanes] = column(weight * (8.0 * d + s * v))
            return carry

        lax.fori_loop(0, MODES // TOGETHER, some, 0, unroll=True)
    parts[0] = sums_s[...].astype(BF16)
    sums[0, 2 * MODES : 3 * MODES, :] = residue[...]


def dft(table, signal):
    return jnp.dot(table, signal, preferred_element_type=F32)


def correlate(forward, inverse, left, right):
    lr, li, rr, ri = left[:LEN], left[LEN:], right[:LEN], right[LEN:]
    both = jnp.concatenate([(lr * rr + li * ri).astype(BF16), (lr * ri - li * rr).astype(BF16)], 0)
    return dft(inverse, both)


def convolve(forward, inverse, left, right):
    lr, li, rr, ri = left[:LEN], left[LEN:], right[:LEN], right[LEN:]
    both = jnp.concatenate([(lr * rr - li * ri).astype(BF16), (lr * ri + li * rr).astype(BF16)], 0)
    return dft(inverse, both)


def lag_kernel(core, forward, inverse, x_keep, g_keep, x_got, g_got, x_out, g_out, lag):
    low = pl.multiple_of(core[0] * HALF, HALF)
    high = pl.multiple_of(HALF - core[0] * HALF, HALF)
    for keep, got, out in ((x_keep, x_got, x_out), (g_keep, g_got, g_out)):
        out[pl.ds(low, HALF), :] = keep[...]
        out[pl.ds(high, HALF), :] = got[...]
    fwd, inv = forward[...], inverse[...]
    lag[...] = correlate(fwd, inv, dft(fwd, x_out[...]), dft(fwd, g_out[...]))


def grad_kernel(prm, lag, grad_a, parts, sums_s):
    for tile in range(WIDTH // 128):
        lanes = pl.ds(128 * tile, 128)
        s = ladder(128)

        def some(group, carry):
            modes = [TOGETHER * group + i for i in range(TOGETHER)]
            rates = [prm[0, pl.ds(m, 1), lanes] for m in modes]
            (lags,) = power_sums(rates, ((lag, False),), lanes)
            for m, rate, (v, d) in zip(modes, rates, lags):
                weight = jnp.exp(-rate * s)
                sums_s[pl.ds(m, 1), lanes] = column(weight * v)
                sums_s[pl.ds(MODES + m, 1), lanes] = column(weight * (8.0 * d + s * v))
            return carry

        lax.fori_loop(0, MODES // TOGETHER, some, 0, unroll=True)
    parts[0, 0:32, :] = grad_a[0]
    parts[0, 32:64, :] = sums_s[...].astype(BF16)


def expand(minus, steps, heads, flip, put, count):
    for tile in range(WIDTH // 128):
        lanes = pl.ds(128 * tile, 128)
        s = ladder(128, flip)
        y = tuple(jnp.broadcast_to(steps[pl.ds(m, 1), lanes], (8, 128)) for m in range(MODES))
        z = tuple(heads[pl.ds(m, 1), lanes] * jnp.exp(minus[pl.ds(m, 1), lanes] * s) for m in range(MODES))
        for k in range(count):
            put(k, lanes, total(z))
            if k < count - 1:
                z = tuple(u * v for u, v in zip(z, y))


def local_kernel(core, prm, residue, forward, inverse, x, g, conv_keep, back_keep, conv_give, back_give, filt_s, minus_s, step_s, res_s):
    fwd, inv = forward[...], inverse[...]
    even = core[0] == 0
    minus_s[...] = -prm[0]
    step_s[...] = jnp.exp(-8.0 * prm[0])
    res_s[...] = residue[0]

    def put(k, lanes, rows):
        filt_s[pl.ds(8 * k, 8), lanes] = rows

    expand(minus_s, step_s, res_s, False, put, STEPS)
    for part in range(WIDTH // PART):
        lanes = pl.ds(PART * part, PART)
        filt = dft(fwd, filt_s[:, lanes].astype(BF16))
        conv = convolve(fwd, inv, filt, dft(fwd, x[:, lanes])).astype(BF16)
        back = correlate(fwd, inv, filt, dft(fwd, g[:, lanes])).astype(BF16)
        for both, keep, give in ((conv, conv_keep, conv_give), (back, back_keep, back_give)):
            keep[:, lanes] = jnp.where(even, both[:HALF], both[HALF:])
            give[:, lanes] = jnp.where(even, both[HALF:], both[:HALF])


def scan_kernel(sums, parts, own_rate, residue, out):
    rate = own_rate[...]
    scale = residue[...] * jnp.exp(-rate)
    far = jnp.exp(-float(LEN) * rate)

    def write(d, base, state):
        ends = scale * state
        near = ends.astype(BF16)
        out[d, base : base + MODES, :] = near
        out[d, base + MODES : base + 2 * MODES, :] = (ends - near.astype(F32)).astype(BF16)

    state = jnp.zeros((MODES, WIDTH), F32)
    for d in range(BLOCKS):
        write(d, 0, state)
        state = far * state + sums[d, 0:MODES, :]
    state = jnp.zeros((MODES, WIDTH), F32)
    for d in range(BLOCKS - 1, -1, -1):
        write(d, 2 * MODES, state)
        state = far * state + sums[d, MODES : 2 * MODES, :]


def owner_grad_kernel(sums, got, own_rate, residue, out):
    rate = own_rate[...]
    lam = jnp.exp(-rate)
    far = jnp.exp(-float(LEN) * rate)
    zero = jnp.zeros((MODES, WIDTH), F32)
    h, q, hg, pg, hb, qb = zero, zero, zero, zero, zero, zero
    for d in range(BLOCKS):
        b = sums[d, MODES : 2 * MODES, :]
        p, w, hd, pd = (got[d, 16 * i : 16 * i + 16, :].astype(F32) for i in range(4))
        hg = hg + hd
        pg = pg + pd
        hb = hb + h * b
        qb = qb + h * (w + b) + q * b
        q = far * (q + float(LEN) * h) + p
        h = far * h + sums[d, 0:MODES, :]
    first = hg + lam * hb
    second = -residue[...] * (pg + lam * qb)
    for b in range(out.shape[0]):
        out[b, 0:MODES, :] = first
        out[b, MODES : 2 * MODES, :] = second


def sum_kernel(grads, residue_grad, rate_grad):
    residue_grad[...] = total(grads[b, 0:MODES, :] for b in range(grads.shape[0]))
    rate_grad[...] = total(grads[b, MODES : 2 * MODES, :] for b in range(grads.shape[0]))


def finish_kernel(
    core, prm, prm_got, ends, ends_got, conv_keep, back_keep, conv_got, back_got, out_grad, keys, values,
    query_out, key_out, value_out, minus_s, step_s, head_s, tail_s, conv_s, back_s,
):
    upper = core[0].astype(F32) * float(HALF)
    for h in range(2):
        mine = core[0] == h
        minus = -jnp.where(mine, prm[0], prm_got[0])
        edge = jnp.where(mine, ends[0], ends_got[0]).astype(F32)
        minus_s[h] = minus
        step_s[h] = jnp.exp(8.0 * minus)
        head_s[h] = (edge[0:16] + edge[16:32]) * jnp.exp(minus * upper)
        tail_s[h] = (edge[32:48] + edge[48:64]) * jnp.exp(minus * (float(HALF) - upper))

        def put_conv(k, lanes, rows):
            conv_s[h, pl.ds(8 * k, 8), lanes] = rows

        def put_back(k, lanes, rows):
            back_s[h, pl.ds(HALF - 8 - 8 * k, 8), lanes] = rows

        expand(minus_s.at[h], step_s.at[h], head_s.at[h], False, put_conv, HALF // 8)
        expand(minus_s.at[h], step_s.at[h], tail_s.at[h], True, put_back, HALF // 8)
        c = (jnp.where(mine, conv_keep[...], conv_got[...]).astype(F32) + conv_s[h]).astype(BF16)
        b = (jnp.where(mine, back_keep[...], back_got[...]).astype(F32) + back_s[h]).astype(BF16)
        lanes = pl.ds(h * WIDTH, WIDTH)
        query_out[:, lanes] = product(out_grad[:, lanes], c)
        key_out[:, lanes] = product(b, values[:, lanes])
        value_out[:, lanes] = product(b, keys[:, lanes])


def call(kernel, name, work, grid, in_specs, out_specs, shapes, scratch, operands, prefetch=True, aliases=None):
    spec = pltpu.PrefetchScalarGridSpec(
        num_scalar_prefetch=1 if prefetch else 0, grid=grid, in_specs=in_specs, out_specs=out_specs, scratch_shapes=scratch
    )
    return pl.pallas_call(
        kernel, grid_spec=spec, out_shape=shapes, compiler_params=params(), cost_estimate=work, name=name,
        input_output_aliases=aliases or {},
    )(*operands)


def swap(array):
    return lax.ppermute(array, "ctx", [(i, i ^ 1) for i in range(2 * BLOCKS)])


def exchange(array):
    groups = [[2 * q + c for q in range(BLOCKS)] for c in range(2)]
    return lax.all_to_all(array, "ctx", split_axis=0, concat_axis=0, axis_index_groups=groups, tiled=True)


def body(queries, keys, values, out_grad, residue, rate):
    chans = queries.shape[2]
    half = chans // 2
    queries2, keys2, values2, out_grad2 = (a.reshape(HALF, chans) for a in (queries, keys, values, out_grad))
    core = (lax.axis_index("ctx") % 2).astype(jnp.int32).reshape(1)
    forward, inverse = tables()
    owned = lambda rows, i=0: pl.BlockSpec((BLOCKS, rows, WIDTH), lambda *_: (0, i, 0))
    shape_payload = jax.ShapeDtypeStruct((BLOCKS, 128, WIDTH), BF16)
    work = LEN * half * MODES
    moved = LEN * half

    part = pl.BlockSpec((HALF, WIDTH), lambda q, *_: (0, q))
    whole = pl.BlockSpec((LEN, WIDTH), lambda q, *_: (0, q))
    own = pl.BlockSpec((MODES, WIDTH), lambda q, *_: (0, 0))
    rows16 = pl.BlockSpec((1, MODES, WIDTH), lambda q, *_: (q, 0, 0))
    rows48 = pl.BlockSpec((1, 48, WIDTH), lambda q, *_: (q, 0, 0))
    residues = pl.BlockSpec((1, MODES, WIDTH), lambda q, *_: (q, 2, 0))
    rows32 = pl.BlockSpec((1, 32, WIDTH), lambda q, *_: (q, 0, 0))
    rows64 = pl.BlockSpec((1, 64, WIDTH), lambda q, *_: (q, 0, 0))
    table_f = pl.BlockSpec((2 * LEN, LEN), lambda q, *_: (0, 0))
    table_i = pl.BlockSpec((LEN, 2 * LEN), lambda q, *_: (0, 0))
    shape_part = jax.ShapeDtypeStruct((HALF, half), BF16)
    shape_whole = jax.ShapeDtypeStruct((LEN, half), BF16)
    shape_rows = jax.ShapeDtypeStruct((BLOCKS, 32, WIDTH), BF16)
    wide = pltpu.VMEM((LEN, WIDTH), F32)
    narrow = pltpu.VMEM((32, WIDTH), F32)

    pair = pl.BlockSpec((HALF, 8 * WIDTH), lambda q, *_: (0, q))
    pair_half = pl.BlockSpec((HALF, 4 * WIDTH), lambda q, *_: (0, q))
    copies, x_keep, g_keep, x_give, g_give = call(
        gate_kernel, "gate", cost(2 * moved, 12 * moved), (BLOCKS // 4,), [own] + [pair] * 4,
        [pl.BlockSpec((BLOCKS, MODES, WIDTH), lambda *_: (0, 0, 0))] + [pair_half] * 4,
        [jax.ShapeDtypeStruct((BLOCKS, MODES, WIDTH), F32)] + [shape_part] * 4, [],
        (core, rate, keys2, values2, out_grad2, queries2),
    )
    prm = exchange(copies)
    x_got, g_got = swap(x_give), swap(g_give)
    double = pl.BlockSpec((HALF, 2 * WIDTH), lambda q, *_: (0, q))
    double_whole = pl.BlockSpec((LEN, 2 * WIDTH), lambda q, *_: (0, q))
    x, g, lag = call(
        lag_kernel, "lags", cost(work, 16 * moved), (BLOCKS // 2,), [table_f, table_i] + [double] * 4,
        [double_whole] * 3, [shape_whole, shape_whole, jax.ShapeDtypeStruct((LEN, half), F32)], [],
        (core, forward, inverse, x_keep, g_keep, x_got, g_got),
    )
    prm_got = swap(prm)
    sums, grad_a = call(
        state_kernel, "states", cost(7 * work, 4 * moved), (BLOCKS,), [rows16, own, whole, whole], [rows48, rows32],
        [jax.ShapeDtypeStruct((BLOCKS, 48, WIDTH), F32), shape_rows], [wide, wide, narrow], (prm, residue, x, g), False,
    )
    sums_own = exchange(sums)
    parts = call(
        grad_kernel, "local_grads", cost(4 * work, 4 * moved), (BLOCKS,), [rows16, whole, rows32],
        pl.BlockSpec((1, 64, WIDTH), lambda q, *_: (q, 1, 0)), shape_payload, [narrow], (prm, lag, grad_a), False,
    )
    prm_got, parts = lax.optimization_barrier((prm_got, parts))
    ends_own = call(
        scan_kernel, "scan", cost(1000, 1000000), (1,), [owned(32), pl.BlockSpec(memory_space=pl.ANY), own, own], owned(64),
        shape_payload, [], (sums_own, parts, rate, residue), False, {1: 0},
    )
    ends = exchange(ends_own)
    few = pltpu.VMEM((MODES, WIDTH), F32)
    conv_keep, back_keep, conv_give, back_give = call(
        local_kernel, "local_conv", cost(5 * work, 8 * moved), (BLOCKS,),
        [rows16, residues, table_f, table_i, whole, whole], [part] * 4, [shape_part] * 4, [wide] + [few] * 3,
        (core, prm, sums_own, forward, inverse, x, g),
    )
    conv_got, back_got = swap(conv_give), swap(back_give)
    ends, conv_keep = lax.optimization_barrier((ends, conv_keep))
    ends_got = swap(ends)
    grads = call(
        owner_grad_kernel, "owner_grads", cost(1000, 2000000), (1,), [owned(32), owned(64, 1), own, own],
        pl.BlockSpec((8, 32, WIDTH), lambda *_: (0, 0, 0)), jax.ShapeDtypeStruct((8, 32, WIDTH), F32), [],
        (sums_own, ends, rate, residue), False,
    )
    grads, ends = lax.optimization_barrier((grads, ends))
    grads = lax.all_to_all(grads, "dp", split_axis=0, concat_axis=0, tiled=True)
    big = pl.BlockSpec((HALF, 2 * WIDTH), lambda q, *_: (0, q))
    pair_specs = [rows16, rows16, rows64, rows64]
    shape_out = jax.ShapeDtypeStruct((HALF, chans), BF16)
    half_wide = pltpu.VMEM((2, HALF, WIDTH), F32)
    few_two = pltpu.VMEM((2, MODES, WIDTH), F32)
    outs = call(
        finish_kernel, "finish", cost(4 * work, 20 * moved), (BLOCKS,),
        pair_specs + [part] * 4 + [big] * 3, [big] * 3, [shape_out] * 3,
        [few_two] * 4 + [half_wide] * 2,
        (core, prm, prm_got, ends, ends_got, conv_keep, back_keep, conv_got, back_got, out_grad2, keys2, values2),
    )
    outs, grads = lax.optimization_barrier((outs, grads))
    residue_grad, rate_grad = pl.pallas_call(
        sum_kernel,
        out_shape=[jax.ShapeDtypeStruct((MODES, WIDTH), F32)] * 2,
        compiler_params=params(),
        name="sum_grads",
    )(grads)
    query_grad, key_grad, value_grad = (a.reshape(queries.shape) for a in outs)
    return query_grad, key_grad, value_grad, residue_grad, rate_grad


def solution(mesh):
    wide = P("dp", "ctx", None)
    narrow = P(None, "ctx")
    return jax.shard_map(
        body,
        mesh=mesh,
        in_specs=(wide,) * 4 + (narrow,) * 2,
        out_specs=(wide,) * 3 + (narrow,) * 2,
        check_vma=False,
    )
```
